512 devices in a mesh: line: 4 (over y), tile: 8 (over x, core), row: 16 (over z).
Axes of the slice: x: 4, y: 4, z: 16, core: 2. Of those that a mesh axis runs over, the one named last changes fastest.
Arguments:
- cells: int32 [65536, 128], P(('line', 'tile', 'row')), may hold values from 0 to 8191
- heights: float32 [65536, 128], P(('line', 'tile', 'row')), may hold values from -24 to 24
- weights: float32 [65536, 128], P(('line', 'tile', 'row')), may hold values from 0.25 to 4
- dest: int32 [65536], P(('line', 'tile', 'row')), may hold values from 0 to 127, as said below
- counts: int32 [4, 8, 16], P('line', 'tile', 'row'), may hold values from 64 to 128, as said below
- prefire_elevation: float32 [1024, 1024], P('row', 'tile'), may hold values from -6 to 6
Outputs:
- elevation_change: float32 [1024, 1024], P('row', 'tile')
The draws below stay inside these ranges and needn't reach their ends.
Inputs may be any that keep to these rules, and one draw needn't show every extreme that they name: `dest`: among the 128 blocks of one device, live or not, at most 2 name any one tile; in every draw one tile is named by exactly 2 blocks of every device. `counts`: the live blocks of a device are its first ones; some device has all its blocks live.
All inputs are finite; a program needn't handle non-finite values.
Results may differ from the reference program's by a relative error of at most 0.0018.
Values sent between devices are 32-bit elements; how exact they have to be, the bound alone decides.
No kernel may reach another device: no remote copies, remote signals or barrier semaphores. Data moves between devices by JAX's collectives and lax.ppermute only.
A program may use at most 64 MiB of HBM per device.

```python
import math
import jax
import jax.numpy as jnp
from jax import lax

BLOCK_SIZE = 128
BLOCKS_DEV = 128
TILE_ROWS = 64
TILE_COLS = 128
TILES = 128
CAPACITY = 2
BLOCKS = 65536
GRID_ROW_COUNT = 1024
GRID_COLUMN_COUNT = 1024
N_LINE = 4
N_TILE = 8
N_ROW = 16


def draw_dest(key, part):
    slots = TILES * CAPACITY
    levels = jax.random.randint(jax.random.fold_in(key, 11), (TILES,), 0, 4)
    heavy = jax.random.randint(jax.random.fold_in(key, 12), (), 0, TILES)
    slot_tile = jnp.arange(slots, dtype=jnp.int32) // CAPACITY
    device_keys = jax.random.split(jax.random.fold_in(key, 13), N_LINE * N_TILE * N_ROW)

    def one_device(device_key):
        noise = jax.random.randint(jax.random.fold_in(device_key, 1), (slots,), 0, 2 ** 19)
        priority = levels[slot_tile] * 2 ** 17 + noise
        priority = jnp.where(slot_tile == heavy, -1, priority)
        score = priority * slots + jnp.arange(slots, dtype=jnp.int32)
        chosen = jax.lax.top_k(-score, BLOCKS_DEV)[1]
        order = jax.random.permutation(jax.random.fold_in(device_key, 2), BLOCKS_DEV)
        return (chosen // CAPACITY)[order].astype(jnp.int32)
    return jax.vmap(one_device)(device_keys).reshape(-1).astype(jnp.int32)


def draw_counts(key, part):
    devices_all = N_LINE * N_TILE * N_ROW
    base = jax.random.randint(jax.random.fold_in(key, 21), (devices_all,), BLOCKS_DEV // 2, BLOCKS_DEV + 1)
    full_at = jax.random.randint(jax.random.fold_in(key, 22), (), 0, devices_all)
    base = jnp.where(jnp.arange(devices_all, dtype=jnp.int32) == full_at, BLOCKS_DEV, base)
    return base.reshape(N_LINE, N_TILE, N_ROW).astype(jnp.int32)


def place_ends(values, key, smallest, top_value):
    longest = values.shape.index(max(values.shape))
    spots = []
    for shift in (0, 1):
        where = [jax.random.randint(jax.random.fold_in(key, axis), (), 0, length) for axis, length in enumerate(values.shape)]
        where[longest] = (where[longest] + shift) % values.shape[longest]
        spots.append(tuple(where))
    return values.at[spots[0]].set(smallest).at[spots[1]].set(top_value)


def steps_of(stream_key, extent, pieces, low, largest):
    level = 1.0
    for axis_at, parts in pieces:
        steps = jax.random.uniform(jax.random.fold_in(jax.random.fold_in(stream_key, 6), axis_at), (parts,), jnp.float32, low / len(pieces), largest / len(pieces))
        level = level * jnp.repeat(jnp.exp(steps), extent[axis_at] // parts).reshape((-1,) + (1,) * (len(extent) - 1 - axis_at))
    return level


def normal_values(key, extent, scale, reach, pieces=(), held_as=jnp.bfloat16):
    array = scale * jax.random.normal(key, extent, jnp.float32)
    if pieces:
        array = array * steps_of(key, extent, pieces, -0.22, 0.18)
    return jnp.clip(array, -reach, reach).astype(held_as)


def setup_inputs(seed: int = 0) -> dict:
    splits = jax.random.split(jax.random.key(seed), 7)
    cells = place_ends(jax.random.randint(splits[0], (BLOCKS, BLOCK_SIZE), 0, TILE_ROWS * TILE_COLS), jax.random.fold_in(splits[0], 1), 0, (TILE_ROWS * TILE_COLS) - 1).astype(jnp.int32)
    heights = normal_values(splits[1], (BLOCKS, BLOCK_SIZE), 4.0, 24.0, ((0, 512),), jnp.float32)
    weights = jnp.clip(jnp.exp(math.log(4.0) - 2.7725887 * jax.random.uniform(splits[2], (BLOCKS, BLOCK_SIZE), jnp.float32) ** steps_of(splits[2], (BLOCKS, BLOCK_SIZE), ((0, 512),), -0.2, 0.2)), 0.25, 4.0)
    dest = draw_dest(jax.random.fold_in(splits[6], 71), 0)
    counts = draw_counts(jax.random.fold_in(splits[6], 71), 0)
    prefire_elevation = normal_values(splits[5], (GRID_ROW_COUNT, GRID_COLUMN_COUNT), 1.0, 6.0, ((0, 16), (1, 8)), jnp.float32)
    return dict(cells=cells, heights=heights, weights=weights, dest=dest, counts=counts, prefire_elevation=prefire_elevation)


def kernel_weight(di, dj):
    if di == 0 and dj == 0:
        return 2.0
    return 1.0 / (di * di + dj * dj)


def reference(cells, heights, weights, dest, counts, prefire_elevation):
    block_ids = jnp.arange(BLOCKS, dtype=jnp.int32)
    owner_counts = counts.reshape(-1)[block_ids // BLOCKS_DEV]
    live = (block_ids % BLOCKS_DEV) < owner_counts
    value_wz = lax.optimization_barrier((weights * heights).astype(jnp.bfloat16)).astype(jnp.float32)
    value_w = lax.optimization_barrier(weights.astype(jnp.bfloat16)).astype(jnp.float32)
    value_wz = jnp.where(live[:, None], value_wz, jnp.float32(0.0))
    value_w = jnp.where(live[:, None], value_w, jnp.float32(0.0))
    tile_row = (dest % N_ROW).astype(jnp.int32)
    tile_col = (dest // N_ROW).astype(jnp.int32)
    grid_row = tile_row[:, None] * TILE_ROWS + cells // TILE_COLS
    grid_col = tile_col[:, None] * TILE_COLS + cells % TILE_COLS
    flat_index = (grid_row * GRID_COLUMN_COUNT + grid_col).reshape(-1)
    sum_wz = jax.ops.segment_sum(value_wz.reshape(-1), flat_index, num_segments=GRID_ROW_COUNT * GRID_COLUMN_COUNT).reshape(GRID_ROW_COUNT, GRID_COLUMN_COUNT)
    sum_w = jax.ops.segment_sum(value_w.reshape(-1), flat_index, num_segments=GRID_ROW_COUNT * GRID_COLUMN_COUNT).reshape(GRID_ROW_COUNT, GRID_COLUMN_COUNT)
    padded_wz = jnp.pad(sum_wz, 2)
    padded_w = jnp.pad(sum_w, 2)
    weighted_height_sum = jnp.zeros((GRID_ROW_COUNT, GRID_COLUMN_COUNT), jnp.float32)
    weight_total = jnp.zeros((GRID_ROW_COUNT, GRID_COLUMN_COUNT), jnp.float32)
    for di in range(-2, 3):
        for dj in range(-2, 3):
            factor = kernel_weight(di, dj)
            weighted_height_sum = weighted_height_sum + factor * padded_wz[2 + di:2 + di + GRID_ROW_COUNT, 2 + dj:2 + dj + GRID_COLUMN_COUNT]
            weight_total = weight_total + factor * padded_w[2 + di:2 + di + GRID_ROW_COUNT, 2 + dj:2 + dj + GRID_COLUMN_COUNT]
    filled_cells = (weighted_height_sum + 16.0 * prefire_elevation) / (weight_total + 16.0)
    return filled_cells - prefire_elevation
```

```python
import jax
import jax.numpy as jnp
from jax import lax
from jax.experimental import pallas as pl
from jax.experimental.pallas import tpu as pltpu
from jax.sharding import PartitionSpec as P

VMEM_SPEC = pl.BlockSpec(memory_space=pltpu.VMEM)
SMEM_SPEC = pl.BlockSpec(memory_space=pltpu.SMEM)
PARAMS = pltpu.CompilerParams(vmem_limit_bytes=40 * 1024 * 1024)
CAPACITY = 2


def call(kernel, out_shape, specs, cost, scratch=()):
    outs = jax.tree.map(lambda _: VMEM_SPEC, out_shape)
    return pl.pallas_call(
        kernel,
        out_shape=out_shape,
        in_specs=specs,
        out_specs=outs,
        scratch_shapes=list(scratch),
        compiler_params=PARAMS,
        cost_estimate=pl.CostEstimate(flops=cost[0], bytes_accessed=cost[1], transcendentals=0),
    )


def pack_kernel(rows, columns, tile_cols, dest_ref, counts_ref, cells_ref, heights_ref, weights_ref, out_ref):
    blocks = cells_ref.shape[0]
    points = cells_ref.shape[1]
    here = columns * CAPACITY
    slots = rows * here
    dest = dest_ref[...]
    across = jnp.broadcast_to(dest.astype(jnp.float32), (blocks, blocks))
    down = across.T
    before = lax.broadcasted_iota(jnp.int32, (blocks, blocks), 0) < lax.broadcasted_iota(
        jnp.int32, (blocks, blocks), 1
    )
    same = jnp.where((across == down) & before, 1.0, 0.0)
    rank = jnp.sum(same, axis=0, keepdims=True).astype(jnp.int32)
    slot = (dest % rows) * here + (dest // rows) * CAPACITY + rank
    live = lax.broadcasted_iota(jnp.int32, (1, blocks), 1) < counts_ref[0, 0]
    slot = jnp.where(live, slot, slots)
    move = jnp.where(
        lax.broadcasted_iota(jnp.int32, (slots, blocks), 0) == slot, 1.0, 0.0
    ).astype(jnp.bfloat16)
    weights = weights_ref[...]
    cells = cells_ref[...]
    payload = jnp.concatenate(
        [
            (weights * heights_ref[...]).astype(jnp.bfloat16),
            weights.astype(jnp.bfloat16),
            (cells // tile_cols).astype(jnp.float32).astype(jnp.bfloat16),
            (cells % tile_cols).astype(jnp.float32).astype(jnp.bfloat16),
        ],
        axis=1,
    )
    moved = jnp.dot(move, payload, preferred_element_type=jnp.float32)
    out_ref[:, 0:here, :] = moved[:, 0:points].reshape(rows, here, points)
    out_ref[:, here : 2 * here, :] = moved[:, points : 2 * points].reshape(rows, here, points)
    cell = moved[:, 2 * points : 3 * points] * tile_cols + moved[:, 3 * points :]
    out_ref[:, 2 * here :, :] = cell.reshape(rows, here, points)


def bin_kernel(columns, tile_rows, tile_cols, in_ref, sums_ref, top_ref, bottom_ref, row_ref, col_ref):
    sources, held, points = in_ref.shape
    here = held // 3
    cells = in_ref[:, 2 * here :, :].astype(jnp.int32)
    row_ref[...] = (cells // tile_cols).astype(jnp.float32)
    col_ref[...] = (cells % tile_cols).astype(jnp.float32)
    row_ids = lax.broadcasted_iota(jnp.int32, (tile_rows, points), 0).astype(jnp.float32).astype(jnp.bfloat16)
    col_ids = lax.broadcasted_iota(jnp.int32, (tile_cols, points), 0).astype(jnp.float32).astype(jnp.bfloat16)
    zero = jnp.zeros((tile_rows, points), jnp.bfloat16)
    one_col = jnp.ones((tile_cols, points), jnp.bfloat16)
    zero_col = jnp.zeros((tile_cols, points), jnp.bfloat16)

    def spread(ref, source, at, count):
        line = ref[source, pl.ds(at, 1), :]
        return jnp.broadcast_to(line, (count, points)).astype(jnp.bfloat16)

    for column in range(columns):
        total = jnp.zeros((2 * tile_rows, tile_cols), jnp.float32)
        for source in range(0, sources, 2):
            lefts, rights = [], []
            for s in (source, source + 1):
                for k in range(CAPACITY):
                    at = column * CAPACITY + k
                    hit = spread(row_ref, s, at, tile_rows) == row_ids
                    wz = spread(in_ref, s, at, tile_rows)
                    w = spread(in_ref, s, here + at, tile_rows)
                    lefts.append(
                        jnp.concatenate([jnp.where(hit, wz, zero), jnp.where(hit, w, zero)], axis=0)
                    )
                    rights.append(
                        jnp.where(spread(col_ref, s, at, tile_cols) == col_ids, one_col, zero_col)
                    )
            total = total + lax.dot_general(
                jnp.concatenate(lefts, axis=1),
                jnp.concatenate(rights, axis=1),
                (((1,), (1,)), ((), ())),
                preferred_element_type=jnp.float32,
            )
        sums_ref[column] = total
        top_ref[column, 0:2, :] = total[0:2, :]
        top_ref[column, 2:4, :] = total[tile_rows : tile_rows + 2, :]
        bottom_ref[column, 0:2, :] = total[tile_rows - 2 : tile_rows, :]
        bottom_ref[column, 2:4, :] = total[2 * tile_rows - 2 :, :]


def stencil_kernel(lines, sums_ref, above_ref, below_ref, out_ref, held_ref, near_ref, far_ref):
    columns, both, tile_cols = sums_ref.shape
    tile_rows = both // 2
    piece = tile_rows // lines
    tall = tile_rows + 16
    lane = lax.broadcasted_iota(jnp.int32, (tall, tile_cols), 1)
    blank = jnp.zeros((tall, tile_cols), jnp.float32)
    for value in range(2):
        for column in range(columns):
            held_ref[column, 0:8, :] = jnp.zeros((8, tile_cols), jnp.float32)
            held_ref[column, tile_rows + 8 :, :] = jnp.zeros((8, tile_cols), jnp.float32)
            held_ref[column, 8 : tile_rows + 8, :] = sums_ref[
                column, value * tile_rows : (value + 1) * tile_rows, :
            ]
            held_ref[column, 6:8, :] = above_ref[column, 2 * value : 2 * value + 2, :]
            held_ref[column, tile_rows + 8 : tile_rows + 10, :] = below_ref[
                column, 2 * value : 2 * value + 2, :
            ]

        def turned(column):
            if column < 0 or column >= columns:
                return blank, blank, blank, blank
            x = held_ref[column]
            return tuple(pltpu.roll(x, s, 1) for s in (1, 2, tile_cols - 1, tile_cols - 2))

        before, here = turned(-1), turned(0)
        for column in range(columns):
            after = turned(column + 1)
            x = held_ref[column]
            one = jnp.where(lane < 1, before[0], here[0]) + jnp.where(
                lane >= tile_cols - 1, after[2], here[2]
            )
            two = jnp.where(lane < 2, before[1], here[1]) + jnp.where(
                lane >= tile_cols - 2, after[3], here[3]
            )
            same = 2.0 * x + one + 0.25 * two
            near_ref[...] = x + 0.5 * one + 0.2 * two
            far_ref[...] = 0.25 * x + 0.2 * one + 0.125 * two
            out = (
                same[8 : tile_rows + 8, :]
                + near_ref[7 : tile_rows + 7, :]
                + near_ref[9 : tile_rows + 9, :]
                + far_ref[6 : tile_rows + 6, :]
                + far_ref[10 : tile_rows + 10, :]
            )
            for line in range(lines):
                out_ref[line * columns + column, value * piece : (value + 1) * piece, :] = out[
                    line * piece : (line + 1) * piece, :
                ]
            before, here = here, after


def finish_kernel(line_ref, parts_ref, prefire_ref, out_ref):
    sources, both, tile_cols = parts_ref.shape
    lines, piece, _ = out_ref.shape
    total = parts_ref[0]
    for source in range(1, sources):
        total = total + parts_ref[source]
    at = pl.multiple_of(line_ref[0, 0] * piece, piece)
    prefire = prefire_ref[pl.ds(at, piece), :]
    filled = (total[:piece] + 16.0 * prefire) / (total[piece:] + 16.0)
    change = filled - prefire
    for line in range(lines):
        out_ref[line] = change


def per_device(cells, heights, weights, dest, counts, prefire_elevation):
    lines, columns, rows = (lax.axis_size(a) for a in ("line", "tile", "row"))
    blocks, points = cells.shape
    tile_rows, tile_cols = prefire_elevation.shape
    here = columns * CAPACITY
    f32 = jnp.float32
    piece = tile_rows // lines

    packed = call(
        lambda *refs: pack_kernel(rows, columns, tile_cols, *refs),
        jax.ShapeDtypeStruct((rows, 3 * here, points), f32),
        [VMEM_SPEC, SMEM_SPEC, VMEM_SPEC, VMEM_SPEC, VMEM_SPEC],
        (2 * rows * here * blocks * 4 * points, 4 * 6 * rows * here * points),
    )(dest.reshape(1, blocks), counts.reshape(1, 1), cells, heights, weights)
    arrived = lax.all_to_all(packed, "row", split_axis=0, concat_axis=0, tiled=True)

    edge = jax.ShapeDtypeStruct((columns, 4, tile_cols), f32)
    sums, top, bottom = call(
        lambda *refs: bin_kernel(columns, tile_rows, tile_cols, *refs),
        [jax.ShapeDtypeStruct((columns, 2 * tile_rows, tile_cols), f32), edge, edge],
        [VMEM_SPEC],
        (4 * rows * here * points * tile_rows * tile_cols, 4 * 4 * rows * here * points),
        [pltpu.VMEM((rows, here, points), f32), pltpu.VMEM((rows, here, points), f32)],
    )(arrived)
    up = [(i, i + 1) for i in range(rows - 1)]
    above = lax.ppermute(bottom, "row", up)
    below = lax.ppermute(top, "row", [(j, i) for i, j in up])

    tall = tile_rows + 16
    parts = call(
        lambda *refs: stencil_kernel(lines, *refs),
        jax.ShapeDtypeStruct((lines * columns, 2 * piece, tile_cols), f32),
        [VMEM_SPEC] * 3,
        (30 * columns * 2 * tile_rows * tile_cols, 4 * 4 * columns * tile_rows * tile_cols),
        [
            pltpu.VMEM((columns, tall, tile_cols), f32),
            pltpu.VMEM((tall, tile_cols), f32),
            pltpu.VMEM((tall, tile_cols), f32),
        ],
    )(sums, above, below)
    gathered = lax.all_to_all(parts, ("line", "tile"), split_axis=0, concat_axis=0, tiled=True)

    mine = lax.axis_index("line").astype(jnp.int32).reshape(1, 1)
    change = call(
        finish_kernel,
        jax.ShapeDtypeStruct((lines, piece, tile_cols), f32),
        [SMEM_SPEC, VMEM_SPEC, VMEM_SPEC],
        (lines * columns * 2 * piece * tile_cols, 4 * lines * columns * 2 * piece * tile_cols),
    )(mine, gathered, prefire_elevation)
    strips = lax.all_to_all(change, "line", split_axis=0, concat_axis=0, tiled=True)
    return strips.reshape(tile_rows, tile_cols)


def solution(mesh):
    placed = (
        P(("line", "tile", "row"), None),
        P(("line", "tile", "row"), None),
        P(("line", "tile", "row"), None),
        P(("line", "tile", "row")),
        P("line", "tile", "row"),
        P("row", "tile"),
    )
    return jax.shard_map(
        per_device, mesh=mesh, in_specs=placed, out_specs=P("row", "tile"), check_vma=False
    )
```

```python
import jax
import jax.numpy as jnp
from jax import lax
from jax.experimental import pallas as pl
from jax.experimental.pallas import tpu as pltpu
from jax.sharding import PartitionSpec as P

VMEM_SPEC = pl.BlockSpec(memory_space=pltpu.VMEM)
HBM_SPEC = pl.BlockSpec(memory_space=pltpu.HBM)
SMEM_SPEC = pl.BlockSpec(memory_space=pltpu.SMEM)
PARAMS = pltpu.CompilerParams(vmem_limit_bytes=40 * 1024 * 1024)
WHOLE_PARAMS = pltpu.CompilerParams(vmem_limit_bytes=60 * 1024 * 1024)
CAPACITY = 2


def call(kernel, out_shape, specs, cost, scratch=(), params=PARAMS):
    outs = jax.tree.map(lambda _: VMEM_SPEC, out_shape)
    return pl.pallas_call(
        kernel,
        out_shape=out_shape,
        in_specs=specs,
        out_specs=outs,
        scratch_shapes=list(scratch),
        compiler_params=params,
        cost_estimate=pl.CostEstimate(flops=cost[0], bytes_accessed=cost[1], transcendentals=0),
    )


def pack_kernel(rows, columns, tile_cols, *refs):
    dest_hbm, counts_ref, cells_hbm, heights_hbm, weights_hbm, out_ref = refs[:6]
    dest_ref, cells_ref, heights_ref, weights_ref, sems = refs[6:]
    copies = [
        pltpu.make_async_copy(source, target, sems.at[i])
        for i, (source, target) in enumerate(
            (
                (dest_hbm, dest_ref),
                (weights_hbm, weights_ref),
                (heights_hbm, heights_ref),
                (cells_hbm, cells_ref),
            )
        )
    ]
    for copy in copies:
        copy.start()
    copies[0].wait()
    blocks = cells_ref.shape[0]
    points = cells_ref.shape[1]
    here = columns * CAPACITY
    slots = rows * here
    dest = dest_ref[...]
    across = jnp.broadcast_to(dest.astype(jnp.float32), (blocks, blocks))
    down = across.T
    before = lax.broadcasted_iota(jnp.int32, (blocks, blocks), 0) < lax.broadcasted_iota(
        jnp.int32, (blocks, blocks), 1
    )
    same = jnp.where((across == down) & before, 1.0, 0.0)
    rank = jnp.sum(same, axis=0, keepdims=True).astype(jnp.int32)
    slot = (dest % rows) * here + (dest // rows) * CAPACITY + rank
    live = lax.broadcasted_iota(jnp.int32, (1, blocks), 1) < counts_ref[0, 0]
    slot = jnp.where(live, slot, slots)
    move = jnp.where(
        lax.broadcasted_iota(jnp.int32, (slots, blocks), 0) == slot, 1.0, 0.0
    ).astype(jnp.bfloat16)
    for copy in copies[1:]:
        copy.wait()
    weights = weights_ref[...]
    cells = cells_ref[...]
    payload = jnp.concatenate(
        [
            (weights * heights_ref[...]).astype(jnp.bfloat16),
            weights.astype(jnp.bfloat16),
            (cells // tile_cols).astype(jnp.float32).astype(jnp.bfloat16),
            (cells % tile_cols).astype(jnp.float32).astype(jnp.bfloat16),
        ],
        axis=1,
    )
    moved = jnp.dot(move, payload, preferred_element_type=jnp.float32)
    out_ref[:, 0:here, :] = moved[:, 0:points].reshape(rows, here, points)
    out_ref[:, here : 2 * here, :] = moved[:, points : 2 * points].reshape(rows, here, points)
    cell = moved[:, 2 * points : 3 * points] * tile_cols + moved[:, 3 * points :]
    out_ref[:, 2 * here :, :] = cell.reshape(rows, here, points)


def bin_kernel(columns, tile_rows, tile_cols, in_ref, sums_ref, top_ref, bottom_ref, row_ref, col_ref):
    sources, held, points = in_ref.shape
    here = held // 3
    cells = in_ref[:, 2 * here :, :].astype(jnp.int32)
    row_ref[...] = (cells // tile_cols).astype(jnp.float32)
    col_ref[...] = (cells % tile_cols).astype(jnp.float32)
    row_ids = lax.broadcasted_iota(jnp.int32, (tile_rows, points), 0).astype(jnp.float32).astype(jnp.bfloat16)
    col_ids = lax.broadcasted_iota(jnp.int32, (tile_cols, points), 0).astype(jnp.float32).astype(jnp.bfloat16)
    zero = jnp.zeros((tile_rows, points), jnp.bfloat16)
    one_col = jnp.ones((tile_cols, points), jnp.bfloat16)
    zero_col = jnp.zeros((tile_cols, points), jnp.bfloat16)

    def spread(ref, source, at, count):
        line = ref[source, pl.ds(at, 1), :]
        return jnp.broadcast_to(line, (count, points)).astype(jnp.bfloat16)

    for column in range(columns):
        total = jnp.zeros((2 * tile_rows, tile_cols), jnp.float32)
        for source in range(0, sources, 2):
            lefts, rights = [], []
            for s in (source, source + 1):
                for k in range(CAPACITY):
                    at = column * CAPACITY + k
                    hit = spread(row_ref, s, at, tile_rows) == row_ids
                    wz = spread(in_ref, s, at, tile_rows)
                    w = spread(in_ref, s, here + at, tile_rows)
                    lefts.append(
                        jnp.concatenate([jnp.where(hit, wz, zero), jnp.where(hit, w, zero)], axis=0)
                    )
                    rights.append(
                        jnp.where(spread(col_ref, s, at, tile_cols) == col_ids, one_col, zero_col)
                    )
            total = total + lax.dot_general(
                jnp.concatenate(lefts, axis=1),
                jnp.concatenate(rights, axis=1),
                (((1,), (1,)), ((), ())),
                preferred_element_type=jnp.float32,
            )
        sums_ref[column] = total
        top_ref[column, 0:2, :] = total[0:2, :]
        top_ref[column, 2:4, :] = total[tile_rows : tile_rows + 2, :]
        bottom_ref[column, 0:2, :] = total[tile_rows - 2 : tile_rows, :]
        bottom_ref[column, 2:4, :] = total[2 * tile_rows - 2 :, :]


def stencil_kernel(lines, sums_ref, out_ref, held_ref, near_ref, far_ref):
    columns, both, tile_cols = sums_ref.shape
    tile_rows = both // 2
    piece = tile_rows // lines
    tall = tile_rows + 16
    lane = lax.broadcasted_iota(jnp.int32, (tall, tile_cols), 1)
    blank = jnp.zeros((tall, tile_cols), jnp.float32)
    for value in range(2):
        for column in range(columns):
            held_ref[column, 0:8, :] = jnp.zeros((8, tile_cols), jnp.float32)
            held_ref[column, tile_rows + 8 :, :] = jnp.zeros((8, tile_cols), jnp.float32)
            held_ref[column, 8 : tile_rows + 8, :] = sums_ref[
                column, value * tile_rows : (value + 1) * tile_rows, :
            ]

        def turned(column):
            if column < 0 or column >= columns:
                return blank, blank, blank, blank
            x = held_ref[column]
            return tuple(pltpu.roll(x, s, 1) for s in (1, 2, tile_cols - 1, tile_cols - 2))

        before, here = turned(-1), turned(0)
        for column in range(columns):
            after = turned(column + 1)
            x = held_ref[column]
            one = jnp.where(lane < 1, before[0], here[0]) + jnp.where(
                lane >= tile_cols - 1, after[2], here[2]
            )
            two = jnp.where(lane < 2, before[1], here[1]) + jnp.where(
                lane >= tile_cols - 2, after[3], here[3]
            )
            same = 2.0 * x + one + 0.25 * two
            near_ref[...] = x + 0.5 * one + 0.2 * two
            far_ref[...] = 0.25 * x + 0.2 * one + 0.125 * two
            out = (
                same[8 : tile_rows + 8, :]
                + near_ref[7 : tile_rows + 7, :]
                + near_ref[9 : tile_rows + 9, :]
                + far_ref[6 : tile_rows + 6, :]
                + far_ref[10 : tile_rows + 10, :]
            )
            for line in range(lines):
                out_ref[line * columns + column, value * piece : (value + 1) * piece, :] = out[
                    line * piece : (line + 1) * piece, :
                ]
            before, here = here, after


def border_kernel(lines, parts_ref, above_ref, below_ref, out_ref):
    columns, held, tile_cols = above_ref.shape
    piece = out_ref.shape[1] // 2
    lane = lax.broadcasted_iota(jnp.int32, (held, tile_cols), 1)
    blank = jnp.zeros((held, tile_cols), jnp.float32)
    out_ref[...] = parts_ref[...]

    def filtered(ref):
        def turned(column):
            if column < 0 or column >= columns:
                return blank, blank, blank, blank
            x = ref[column]
            return tuple(pltpu.roll(x, s, 1) for s in (1, 2, tile_cols - 1, tile_cols - 2))

        before, here = turned(-1), turned(0)
        for column in range(columns):
            after = turned(column + 1)
            x = ref[column]
            one = jnp.where(lane < 1, before[0], here[0]) + jnp.where(
                lane >= tile_cols - 1, after[2], here[2]
            )
            two = jnp.where(lane < 2, before[1], here[1]) + jnp.where(
                lane >= tile_cols - 2, after[3], here[3]
            )
            yield column, x + 0.5 * one + 0.2 * two, 0.25 * x + 0.2 * one + 0.125 * two
            before, here = here, after

    def add(at, row, value):
        out_ref[at, row : row + 1, :] = parts_ref[at, row : row + 1, :] + value

    for column, near, far in filtered(above_ref):
        for value in range(2):
            r = 2 * value
            add(column, value * piece, far[r : r + 1] + near[r + 1 : r + 2])
            add(column, value * piece + 1, far[r + 1 : r + 2])
    last = (lines - 1) * columns
    for column, near, far in filtered(below_ref):
        for value in range(2):
            r = 2 * value
            add(last + column, (value + 1) * piece - 2, far[r : r + 1])
            add(last + column, (value + 1) * piece - 1, near[r : r + 1] + far[r + 1 : r + 2])


def finish_kernel(line_ref, parts_ref, prefire_ref, out_ref):
    sources, both, tile_cols = parts_ref.shape
    lines, piece, _ = out_ref.shape
    total = parts_ref[0]
    for source in range(1, sources):
        total = total + parts_ref[source]
    at = pl.multiple_of(line_ref[0, 0] * piece, piece)
    prefire = prefire_ref[pl.ds(at, piece), :]
    filled = (total[:piece] + 16.0 * prefire) / (total[piece:] + 16.0)
    change = filled - prefire
    for line in range(lines):
        out_ref[line] = change


def per_device(cells, heights, weights, dest, counts, prefire_elevation):
    lines, columns, rows = (lax.axis_size(a) for a in ("line", "tile", "row"))
    blocks, points = cells.shape
    tile_rows, tile_cols = prefire_elevation.shape
    here = columns * CAPACITY
    f32 = jnp.float32
    piece = tile_rows // lines

    packed = call(
        lambda *refs: pack_kernel(rows, columns, tile_cols, *refs),
        jax.ShapeDtypeStruct((rows, 3 * here, points), f32),
        [HBM_SPEC, SMEM_SPEC, HBM_SPEC, HBM_SPEC, HBM_SPEC],
        (2 * rows * here * blocks * 4 * points, 4 * 6 * rows * here * points),
        [
            pltpu.VMEM((1, blocks), jnp.int32),
            pltpu.VMEM((blocks, points), jnp.int32),
            pltpu.VMEM((blocks, points), f32),
            pltpu.VMEM((blocks, points), f32),
            pltpu.SemaphoreType.DMA((4,)),
        ],
        params=WHOLE_PARAMS,
    )(dest.reshape(1, blocks), counts.reshape(1, 1), cells, heights, weights)
    arrived = lax.all_to_all(packed, "row", split_axis=0, concat_axis=0, tiled=True)

    edge = jax.ShapeDtypeStruct((columns, 4, tile_cols), f32)
    sums, top, bottom = call(
        lambda *refs: bin_kernel(columns, tile_rows, tile_cols, *refs),
        [jax.ShapeDtypeStruct((columns, 2 * tile_rows, tile_cols), f32), edge, edge],
        [VMEM_SPEC],
        (4 * rows * here * points * tile_rows * tile_cols, 4 * 4 * rows * here * points),
        [pltpu.VMEM((rows, here, points), f32), pltpu.VMEM((rows, here, points), f32)],
    )(arrived)
    up = [(i, i + 1) for i in range(rows - 1)]
    above = lax.ppermute(bottom, "row", up)
    below = lax.ppermute(top, "row", [(j, i) for i, j in up])

    tall = tile_rows + 16
    parts = call(
        lambda *refs: stencil_kernel(lines, *refs),
        jax.ShapeDtypeStruct((lines * columns, 2 * piece, tile_cols), f32),
        [VMEM_SPEC],
        (60 * columns * 2 * tile_rows * tile_cols, 8 * 4 * columns * tile_rows * tile_cols),
        [
            pltpu.VMEM((columns, tall, tile_cols), f32),
            pltpu.VMEM((tall, tile_cols), f32),
            pltpu.VMEM((tall, tile_cols), f32),
        ],
    )(sums)
    parts = call(
        lambda *refs: border_kernel(lines, *refs),
        jax.ShapeDtypeStruct((lines * columns, 2 * piece, tile_cols), f32),
        [VMEM_SPEC] * 3,
        (30 * columns * 8 * tile_cols, 16 * columns * 8 * tile_cols),
    )(parts, above, below)
    gathered = lax.all_to_all(parts, ("line", "tile"), split_axis=0, concat_axis=0, tiled=True)

    mine = lax.axis_index("line").astype(jnp.int32).reshape(1, 1)
    change = call(
        finish_kernel,
        jax.ShapeDtypeStruct((lines, piece, tile_cols), f32),
        [SMEM_SPEC, VMEM_SPEC, VMEM_SPEC],
        (lines * columns * 2 * piece * tile_cols, 4 * lines * columns * 2 * piece * tile_cols),
    )(mine, gathered, prefire_elevation)
    strips = lax.all_to_all(change, "line", split_axis=0, concat_axis=0, tiled=True)
    return strips.reshape(tile_rows, tile_cols)


def solution(mesh):
    placed = (
        P(("line", "tile", "row"), None),
        P(("line", "tile", "row"), None),
        P(("line", "tile", "row"), None),
        P(("line", "tile", "row")),
        P("line", "tile", "row"),
        P("row", "tile"),
    )
    return jax.shard_map(
        per_device, mesh=mesh, in_specs=placed, out_specs=P("row", "tile"), check_vma=False
    )
```

```python
import jax
import jax.numpy as jnp
from jax import lax
from jax.experimental import pallas as pl
from jax.experimental.pallas import tpu as pltpu
from jax.sharding import PartitionSpec as P

VMEM_SPEC = pl.BlockSpec(memory_space=pltpu.VMEM)
HBM_SPEC = pl.BlockSpec(memory_space=pltpu.HBM)
SMEM_SPEC = pl.BlockSpec(memory_space=pltpu.SMEM)
PARAMS = pltpu.CompilerParams(vmem_limit_bytes=40 * 1024 * 1024)
WHOLE_PARAMS = pltpu.CompilerParams(vmem_limit_bytes=60 * 1024 * 1024)
CAPACITY = 2


def call(kernel, out_shape, specs, cost, scratch=(), params=PARAMS, out=VMEM_SPEC):
    outs = jax.tree.map(lambda _: out, out_shape)
    return pl.pallas_call(
        kernel,
        out_shape=out_shape,
        in_specs=specs,
        out_specs=outs,
        scratch_shapes=list(scratch),
        compiler_params=params,
        cost_estimate=pl.CostEstimate(flops=cost[0], bytes_accessed=cost[1], transcendentals=0),
    )


def pack_kernel(rows, columns, tile_cols, *refs):
    dest_hbm, counts_ref, cells_hbm, heights_hbm, weights_hbm, out_ref = refs[:6]
    dest_ref, cells_ref, heights_ref, weights_ref, sems = refs[6:]
    copies = [
        pltpu.make_async_copy(source, target, sems.at[i])
        for i, (source, target) in enumerate(
            (
                (dest_hbm, dest_ref),
                (weights_hbm, weights_ref),
                (heights_hbm, heights_ref),
                (cells_hbm, cells_ref),
            )
        )
    ]
    for copy in copies:
        copy.start()
    copies[0].wait()
    blocks = cells_ref.shape[0]
    points = cells_ref.shape[1]
    here = columns * CAPACITY
    slots = rows * here
    dest = dest_ref[...]
    across = jnp.broadcast_to(dest.astype(jnp.float32), (blocks, blocks))
    down = across.T
    before = lax.broadcasted_iota(jnp.int32, (blocks, blocks), 0) < lax.broadcasted_iota(
        jnp.int32, (blocks, blocks), 1
    )
    same = jnp.where((across == down) & before, 1.0, 0.0)
    rank = jnp.sum(same, axis=0, keepdims=True).astype(jnp.int32)
    slot = (dest % rows) * here + (dest // rows) * CAPACITY + rank
    live = lax.broadcasted_iota(jnp.int32, (1, blocks), 1) < counts_ref[0, 0]
    slot = jnp.where(live, slot, slots)
    move = jnp.where(
        lax.broadcasted_iota(jnp.int32, (slots, blocks), 0) == slot, 1.0, 0.0
    ).astype(jnp.bfloat16)
    for copy in copies[1:]:
        copy.wait()
    weights = weights_ref[...]
    cells = cells_ref[...]
    payload = jnp.concatenate(
        [
            (weights * heights_ref[...]).astype(jnp.bfloat16),
            weights.astype(jnp.bfloat16),
            (cells // tile_cols).astype(jnp.float32).astype(jnp.bfloat16),
            (cells % tile_cols).astype(jnp.float32).astype(jnp.bfloat16),
        ],
        axis=1,
    )
    moved = jnp.dot(move, payload, preferred_element_type=jnp.float32)
    out_ref[:, 0:here, :] = moved[:, 0:points].reshape(rows, here, points)
    out_ref[:, here : 2 * here, :] = moved[:, points : 2 * points].reshape(rows, here, points)
    cell = moved[:, 2 * points : 3 * points] * tile_cols + moved[:, 3 * points :]
    out_ref[:, 2 * here :, :] = cell.reshape(rows, here, points)


def strip_kernel(lines, columns, tile_rows, tile_cols, in_ref, out_hbm, *scratch):
    row_ref, col_ref, held_ref, near_ref, far_ref, out_ref, sems = scratch
    sources, held, points = in_ref.shape
    here = held // 3
    piece = tile_rows // lines
    tall = tile_rows + 16
    first, end = 8, 8 + tile_rows
    cells = in_ref[:, 2 * here :, :].astype(jnp.int32)
    row_ref[...] = (cells // tile_cols).astype(jnp.float32)
    col_ref[...] = (cells % tile_cols).astype(jnp.float32)
    row_ids = lax.broadcasted_iota(jnp.int32, (tile_rows, points), 0)
    row_ids = row_ids.astype(jnp.float32).astype(jnp.bfloat16)
    col_ids = lax.broadcasted_iota(jnp.int32, (tile_cols, points), 0)
    col_ids = col_ids.astype(jnp.float32).astype(jnp.bfloat16)
    zero = jnp.zeros((tile_rows, points), jnp.bfloat16)
    one_col = jnp.ones((tile_cols, points), jnp.bfloat16)
    zero_col = jnp.zeros((tile_cols, points), jnp.bfloat16)
    lane = lax.broadcasted_iota(jnp.int32, (tall, tile_cols), 1)
    blank = jnp.zeros((tall, tile_cols), jnp.float32)
    margin = jnp.zeros((8, tile_cols), jnp.float32)

    def spread(ref, source, at, count):
        line = ref[source, pl.ds(at, 1), :]
        return jnp.broadcast_to(line, (count, points)).astype(jnp.bfloat16)

    def add_up(column):
        total = jnp.zeros((2 * tile_rows, tile_cols), jnp.float32)
        for source in range(0, sources, 2):
            lefts, rights = [], []
            for s in (source, source + 1):
                for k in range(CAPACITY):
                    at = column * CAPACITY + k
                    hit = spread(row_ref, s, at, tile_rows) == row_ids
                    wz = spread(in_ref, s, at, tile_rows)
                    w = spread(in_ref, s, here + at, tile_rows)
                    lefts.append(
                        jnp.concatenate([jnp.where(hit, wz, zero), jnp.where(hit, w, zero)], axis=0)
                    )
                    rights.append(
                        jnp.where(spread(col_ref, s, at, tile_cols) == col_ids, one_col, zero_col)
                    )
            total = total + lax.dot_general(
                jnp.concatenate(lefts, axis=1),
                jnp.concatenate(rights, axis=1),
                (((1,), (1,)), ((), ())),
                preferred_element_type=jnp.float32,
            )
        for value in range(2):
            held_ref[value, column, 0:first, :] = margin
            held_ref[value, column, first:end, :] = total[
                value * tile_rows : (value + 1) * tile_rows, :
            ]
            held_ref[value, column, end:, :] = margin

    def turned(value, column):
        if column < 0 or column >= columns:
            return blank, blank, blank, blank
        x = held_ref[value, column]
        return tuple(pltpu.roll(x, s, 1) for s in (1, 2, tile_cols - 1, tile_cols - 2))

    def filter_column(value, column, before, here, after):
        x = held_ref[value, column]
        one = jnp.where(lane < 1, before[0], here[0]) + jnp.where(
            lane >= tile_cols - 1, after[2], here[2]
        )
        two = jnp.where(lane < 2, before[1], here[1]) + jnp.where(
            lane >= tile_cols - 2, after[3], here[3]
        )
        same = 2.0 * x + one + 0.25 * two
        near_ref[value] = x + 0.5 * one + 0.2 * two
        far_ref[value] = 0.25 * x + 0.2 * one + 0.125 * two

        def near(at, count):
            return near_ref[value, at : at + count, :]

        def far(at, count):
            return far_ref[value, at : at + count, :]

        inner = (
            same[first:end, :]
            + near(first - 1, tile_rows)
            + near(first + 1, tile_rows)
            + far(first - 2, tile_rows)
            + far(first + 2, tile_rows)
        )
        outer = jnp.concatenate(
            [
                far(first, 1),
                near(first, 1) + far(first + 1, 1),
                near(end - 1, 1) + far(end - 2, 1),
                far(end - 1, 1),
            ],
            axis=0,
        )
        base = 2 * piece + 2 * value
        for line in range(lines):
            out_ref[line, column, value * piece : (value + 1) * piece, :] = inner[
                line * piece : (line + 1) * piece, :
            ]
            out_ref[line, column, base : base + 2, :] = outer[0:2]
            out_ref[line, column, base + 4 : base + 6, :] = outer[2:4]

    copies = []
    add_up(0)
    before = [turned(value, -1) for value in range(2)]
    here_now = [turned(value, 0) for value in range(2)]
    for column in range(columns):
        if column + 1 < columns:
            add_up(column + 1)
        after = [turned(value, column + 1) for value in range(2)]
        for value in range(2):
            filter_column(value, column, before[value], here_now[value], after[value])
        before, here_now = here_now, after
        copy = pltpu.make_async_copy(out_ref.at[:, column], out_hbm.at[:, column], sems.at[column])
        copy.start()
        copies.append(copy)
    for copy in copies:
        copy.wait()


def gather_kernel(parts_ref, strips_ref, above_ref, below_ref):
    sources = parts_ref.shape[0]
    lines, both, _ = strips_ref.shape
    total = parts_ref[0]
    for source in range(1, sources):
        total = total + parts_ref[source]
    for line in range(lines):
        strips_ref[line] = total[:both]
    above_ref[...] = total[both : both + 4]
    below_ref[...] = total[both + 4 :]


def finish_kernel(strips_ref, top_ref, bottom_ref, prefire_ref, out_ref, wz_ref, w_ref):
    lines, both, _ = strips_ref.shape
    piece = both // 2
    rows = lines * piece
    for value, ref in enumerate((wz_ref, w_ref)):
        for line in range(lines):
            ref[line * piece : (line + 1) * piece, :] = strips_ref[
                line, value * piece : (value + 1) * piece, :
            ]
        ref[0:2, :] = ref[0:2, :] + top_ref[2 * value : 2 * value + 2, :]
        ref[rows - 2 :, :] = ref[rows - 2 :, :] + bottom_ref[2 * value : 2 * value + 2, :]
    prefire = prefire_ref[...]
    filled = (wz_ref[...] + 16.0 * prefire) / (w_ref[...] + 16.0)
    out_ref[...] = filled - prefire


def per_device(cells, heights, weights, dest, counts, prefire_elevation):
    lines, columns, rows = (lax.axis_size(a) for a in ("line", "tile", "row"))
    blocks, points = cells.shape
    tile_rows, tile_cols = prefire_elevation.shape
    here = columns * CAPACITY
    f32 = jnp.float32
    piece = tile_rows // lines

    packed = call(
        lambda *refs: pack_kernel(rows, columns, tile_cols, *refs),
        jax.ShapeDtypeStruct((rows, 3 * here, points), f32),
        [HBM_SPEC, SMEM_SPEC, HBM_SPEC, HBM_SPEC, HBM_SPEC],
        (2 * rows * here * blocks * 4 * points, 4 * 6 * rows * here * points),
        [
            pltpu.VMEM((1, blocks), jnp.int32),
            pltpu.VMEM((blocks, points), jnp.int32),
            pltpu.VMEM((blocks, points), f32),
            pltpu.VMEM((blocks, points), f32),
            pltpu.SemaphoreType.DMA((4,)),
        ],
        params=WHOLE_PARAMS,
    )(dest.reshape(1, blocks), counts.reshape(1, 1), cells, heights, weights)
    arrived = lax.all_to_all(packed, "row", split_axis=0, concat_axis=0, tiled=True)

    tall = tile_rows + 16
    slot = 2 * piece + 8
    parts = call(
        lambda *refs: strip_kernel(lines, columns, tile_rows, tile_cols, *refs),
        jax.ShapeDtypeStruct((lines, columns, slot, tile_cols), f32),
        [VMEM_SPEC],
        (4 * rows * here * points * tile_rows * tile_cols, 4 * 4 * rows * here * points),
        [
            pltpu.VMEM((rows, here, points), f32),
            pltpu.VMEM((rows, here, points), f32),
            pltpu.VMEM((2, columns, tall, tile_cols), f32),
            pltpu.VMEM((2, tall, tile_cols), f32),
            pltpu.VMEM((2, tall, tile_cols), f32),
            pltpu.VMEM((lines, columns, slot, tile_cols), f32),
            pltpu.SemaphoreType.DMA((columns,)),
        ],
        out=HBM_SPEC,
    )(arrived)
    gathered = lax.all_to_all(
        parts.reshape(lines * columns, slot, tile_cols),
        ("line", "tile"),
        split_axis=0,
        concat_axis=0,
        tiled=True,
    )

    edge = jax.ShapeDtypeStruct((4, tile_cols), f32)
    strips, above, below = call(
        gather_kernel,
        [jax.ShapeDtypeStruct((lines, 2 * piece, tile_cols), f32), edge, edge],
        [VMEM_SPEC],
        (lines * columns * slot * tile_cols, 4 * lines * columns * slot * tile_cols),
    )(gathered)
    up = [(i, i + 1) for i in range(rows - 1)]
    top = lax.ppermute(below, "row", up)
    bottom = lax.ppermute(above, "row", [(j, i) for i, j in up])
    strips = lax.all_to_all(strips, "line", split_axis=0, concat_axis=0, tiled=True)

    return call(
        finish_kernel,
        jax.ShapeDtypeStruct((tile_rows, tile_cols), f32),
        [VMEM_SPEC] * 4,
        (8 * tile_rows * tile_cols, 16 * tile_rows * tile_cols),
        [pltpu.VMEM((tile_rows, tile_cols), f32), pltpu.VMEM((tile_rows, tile_cols), f32)],
    )(strips, top, bottom, prefire_elevation)


def solution(mesh):
    placed = (
        P(("line", "tile", "row"), None),
        P(("line", "tile", "row"), None),
        P(("line", "tile", "row"), None),
        P(("line", "tile", "row")),
        P("line", "tile", "row"),
        P("row", "tile"),
    )
    return jax.shard_map(
        per_device, mesh=mesh, in_specs=placed, out_specs=P("row", "tile"), check_vma=False
    )
```

```python
import jax
import jax.numpy as jnp
from jax import lax
from jax.experimental import pallas as pl
from jax.experimental.pallas import tpu as pltpu
from jax.sharding import Mesh
from jax.sharding import PartitionSpec as P

VMEM_SPEC = pl.BlockSpec(memory_space=pltpu.VMEM)
HBM_SPEC = pl.BlockSpec(memory_space=pltpu.HBM)
SMEM_SPEC = pl.BlockSpec(memory_space=pltpu.SMEM)
PARAMS = pltpu.CompilerParams(vmem_limit_bytes=40 * 1024 * 1024)
WHOLE_PARAMS = pltpu.CompilerParams(vmem_limit_bytes=60 * 1024 * 1024)
CAPACITY = 2
ROW = ("pair", "side")


def call(kernel, out_shape, specs, cost, scratch=(), params=PARAMS, out=VMEM_SPEC):
    outs = jax.tree.map(lambda _: out, out_shape)
    return pl.pallas_call(
        kernel,
        out_shape=out_shape,
        in_specs=specs,
        out_specs=outs,
        scratch_shapes=list(scratch),
        compiler_params=params,
        cost_estimate=pl.CostEstimate(flops=cost[0], bytes_accessed=cost[1], transcendentals=0),
    )


def pack_kernel(rows, columns, tile_cols, *refs):
    dest_hbm, counts_ref, cells_hbm, heights_hbm, weights_hbm, out_ref = refs[:6]
    dest_ref, cells_ref, heights_ref, weights_ref, sems = refs[6:]
    copies = [
        pltpu.make_async_copy(source, target, sems.at[i])
        for i, (source, target) in enumerate(
            (
                (dest_hbm, dest_ref),
                (weights_hbm, weights_ref),
                (heights_hbm, heights_ref),
                (cells_hbm, cells_ref),
            )
        )
    ]
    for copy in copies:
        copy.start()
    copies[0].wait()
    blocks = cells_ref.shape[0]
    points = cells_ref.shape[1]
    here = columns * CAPACITY
    slots = rows * here
    dest = dest_ref[...]
    across = jnp.broadcast_to(dest.astype(jnp.float32), (blocks, blocks))
    down = across.T
    before = lax.broadcasted_iota(jnp.int32, (blocks, blocks), 0) < lax.broadcasted_iota(
        jnp.int32, (blocks, blocks), 1
    )
    same = jnp.where((across == down) & before, 1.0, 0.0)
    rank = jnp.sum(same, axis=0, keepdims=True).astype(jnp.int32)
    slot = (dest % rows) * here + (dest // rows) * CAPACITY + rank
    live = lax.broadcasted_iota(jnp.int32, (1, blocks), 1) < counts_ref[0, 0]
    slot = jnp.where(live, slot, slots)
    move = jnp.where(
        lax.broadcasted_iota(jnp.int32, (slots, blocks), 0) == slot, 1.0, 0.0
    ).astype(jnp.bfloat16)
    for copy in copies[1:]:
        copy.wait()
    weights = weights_ref[...]
    cells = cells_ref[...]
    payload = jnp.concatenate(
        [
            (weights * heights_ref[...]).astype(jnp.bfloat16),
            weights.astype(jnp.bfloat16),
            (cells // tile_cols).astype(jnp.float32).astype(jnp.bfloat16),
            (cells % tile_cols).astype(jnp.float32).astype(jnp.bfloat16),
        ],
        axis=1,
    )
    moved = jnp.dot(move, payload, preferred_element_type=jnp.float32)
    out_ref[:, 0:here, :] = moved[:, 0:points].reshape(rows, here, points)
    out_ref[:, here : 2 * here, :] = moved[:, points : 2 * points].reshape(rows, here, points)
    cell = moved[:, 2 * points : 3 * points] * tile_cols + moved[:, 3 * points :]
    out_ref[:, 2 * here :, :] = cell.reshape(rows, here, points)


def strip_kernel(lines, columns, tile_rows, tile_cols, in_ref, out_hbm, *scratch):
    row_ref, col_ref, held_ref, near_ref, far_ref, out_ref, sems = scratch
    sources, held, points = in_ref.shape
    here = held // 3
    piece = tile_rows // lines
    tall = tile_rows + 16
    first, end = 8, 8 + tile_rows
    cells = in_ref[:, 2 * here :, :].astype(jnp.int32)
    row_ref[...] = (cells // tile_cols).astype(jnp.float32)
    col_ref[...] = (cells % tile_cols).astype(jnp.float32)
    row_ids = lax.broadcasted_iota(jnp.int32, (tile_rows, points), 0)
    row_ids = row_ids.astype(jnp.float32).astype(jnp.bfloat16)
    col_ids = lax.broadcasted_iota(jnp.int32, (tile_cols, points), 0)
    col_ids = col_ids.astype(jnp.float32).astype(jnp.bfloat16)
    zero = jnp.zeros((tile_rows, points), jnp.bfloat16)
    one_col = jnp.ones((tile_cols, points), jnp.bfloat16)
    zero_col = jnp.zeros((tile_cols, points), jnp.bfloat16)
    lane = lax.broadcasted_iota(jnp.int32, (tall, tile_cols), 1)
    blank = jnp.zeros((tall, tile_cols), jnp.float32)
    margin = jnp.zeros((8, tile_cols), jnp.float32)

    def spread(ref, source, at, count):
        line = ref[source, pl.ds(at, 1), :]
        return jnp.broadcast_to(line, (count, points)).astype(jnp.bfloat16)

    def add_up(column):
        total = jnp.zeros((2 * tile_rows, tile_cols), jnp.float32)
        for source in range(0, sources, 2):
            lefts, rights = [], []
            for s in (source, source + 1):
                for k in range(CAPACITY):
                    at = column * CAPACITY + k
                    hit = spread(row_ref, s, at, tile_rows) == row_ids
                    wz = spread(in_ref, s, at, tile_rows)
                    w = spread(in_ref, s, here + at, tile_rows)
                    lefts.append(
                        jnp.concatenate([jnp.where(hit, wz, zero), jnp.where(hit, w, zero)], axis=0)
                    )
                    rights.append(
                        jnp.where(spread(col_ref, s, at, tile_cols) == col_ids, one_col, zero_col)
                    )
            total = total + lax.dot_general(
                jnp.concatenate(lefts, axis=1),
                jnp.concatenate(rights, axis=1),
                (((1,), (1,)), ((), ())),
                preferred_element_type=jnp.float32,
            )
        for value in range(2):
            held_ref[value, column, 0:first, :] = margin
            held_ref[value, column, first:end, :] = total[
                value * tile_rows : (value + 1) * tile_rows, :
            ]
            held_ref[value, column, end:, :] = margin

    def turned(value, column):
        if column < 0 or column >= columns:
            return blank, blank, blank, blank
        x = held_ref[value, column]
        return tuple(pltpu.roll(x, s, 1) for s in (1, 2, tile_cols - 1, tile_cols - 2))

    def filter_column(value, column, before, here, after):
        x = held_ref[value, column]
        one = jnp.where(lane < 1, before[0], here[0]) + jnp.where(
            lane >= tile_cols - 1, after[2], here[2]
        )
        two = jnp.where(lane < 2, before[1], here[1]) + jnp.where(
            lane >= tile_cols - 2, after[3], here[3]
        )
        same = 2.0 * x + one + 0.25 * two
        near_ref[value] = x + 0.5 * one + 0.2 * two
        far_ref[value] = 0.25 * x + 0.2 * one + 0.125 * two

        def near(at, count):
            return near_ref[value, at : at + count, :]

        def far(at, count):
            return far_ref[value, at : at + count, :]

        inner = (
            same[first:end, :]
            + near(first - 1, tile_rows)
            + near(first + 1, tile_rows)
            + far(first - 2, tile_rows)
            + far(first + 2, tile_rows)
        )
        outer = jnp.concatenate(
            [
                far(first, 1),
                near(first, 1) + far(first + 1, 1),
                near(end - 1, 1) + far(end - 2, 1),
                far(end - 1, 1),
            ],
            axis=0,
        )
        base = 2 * piece + 2 * value
        for line in range(lines):
            out_ref[line, column, value * piece : (value + 1) * piece, :] = inner[
                line * piece : (line + 1) * piece, :
            ]
            out_ref[line, column, base : base + 2, :] = outer[0:2]
            out_ref[line, column, base + 4 : base + 6, :] = outer[2:4]

    add_up(0)
    before = [turned(value, -1) for value in range(2)]
    here_now = [turned(value, 0) for value in range(2)]
    for column in range(columns):
        if column + 1 < columns:
            add_up(column + 1)
        after = [turned(value, column + 1) for value in range(2)]
        for value in range(2):
            filter_column(value, column, before[value], here_now[value], after[value])
        before, here_now = here_now, after
    copy = pltpu.make_async_copy(out_ref, out_hbm, sems.at[0])
    copy.start()
    copy.wait()


def gather_kernel(side_ref, parts_ref, strips_ref, cross_ref):
    sources = parts_ref.shape[0]
    ends, both, tile_cols = strips_ref.shape
    total = parts_ref[0]
    for source in range(1, sources):
        total = total + parts_ref[source]
    above = total[both : both + 4]
    below = total[both + 4 :]
    side = side_ref[0, 0]
    lower = side == 0
    partner = jnp.concatenate(
        [jnp.where(lower, below, above), jnp.zeros((both - 4, tile_cols), jnp.float32)], axis=0
    )
    for line in range(ends // 2):
        strips_ref[2 * line + side] = total[:both]
        strips_ref[2 * line + 1 - side] = partner
    cross_ref[...] = jnp.where(lower, above, below)


def finish_kernel(side_ref, strips_ref, cross_ref, prefire_ref, out_ref, wz_ref, w_ref):
    ends, both, _ = strips_ref.shape
    lines = ends // 2
    piece = both // 2
    rows = lines * piece
    side = side_ref[0, 0]
    partner = strips_ref[1 - side, 0:4, :]
    cross = cross_ref[...]
    top = jnp.where(side == 0, cross, partner)
    bottom = jnp.where(side == 0, partner, cross)
    for value, ref in enumerate((wz_ref, w_ref)):
        for line in range(lines):
            ref[line * piece : (line + 1) * piece, :] = strips_ref[
                2 * line + side, value * piece : (value + 1) * piece, :
            ]
        ref[0:2, :] = ref[0:2, :] + top[2 * value : 2 * value + 2]
        ref[rows - 2 :, :] = ref[rows - 2 :, :] + bottom[2 * value : 2 * value + 2]
    prefire = prefire_ref[...]
    filled = (wz_ref[...] + 16.0 * prefire) / (w_ref[...] + 16.0)
    out_ref[...] = filled - prefire


def per_device(cells, heights, weights, dest, counts, prefire_elevation):
    lines, columns, rows = (lax.axis_size(a) for a in ("line", "tile", ROW))
    blocks, points = cells.shape
    tile_rows, tile_cols = prefire_elevation.shape
    here = columns * CAPACITY
    f32 = jnp.float32
    piece = tile_rows // lines

    packed = call(
        lambda *refs: pack_kernel(rows, columns, tile_cols, *refs),
        jax.ShapeDtypeStruct((rows, 3 * here, points), f32),
        [HBM_SPEC, SMEM_SPEC, HBM_SPEC, HBM_SPEC, HBM_SPEC],
        (2 * rows * here * blocks * 4 * points, 4 * 6 * rows * here * points),
        [
            pltpu.VMEM((1, blocks), jnp.int32),
            pltpu.VMEM((blocks, points), jnp.int32),
            pltpu.VMEM((blocks, points), f32),
            pltpu.VMEM((blocks, points), f32),
            pltpu.SemaphoreType.DMA((4,)),
        ],
        params=WHOLE_PARAMS,
    )(dest.reshape(1, blocks), counts.reshape(1, 1), cells, heights, weights)
    arrived = lax.all_to_all(packed, ROW, split_axis=0, concat_axis=0, tiled=True)

    tall = tile_rows + 16
    slot = 2 * piece + 8
    parts = call(
        lambda *refs: strip_kernel(lines, columns, tile_rows, tile_cols, *refs),
        jax.ShapeDtypeStruct((lines, columns, slot, tile_cols), f32),
        [VMEM_SPEC],
        (4 * rows * here * points * tile_rows * tile_cols, 4 * 4 * rows * here * points),
        [
            pltpu.VMEM((rows, here, points), f32),
            pltpu.VMEM((rows, here, points), f32),
            pltpu.VMEM((2, columns, tall, tile_cols), f32),
            pltpu.VMEM((2, tall, tile_cols), f32),
            pltpu.VMEM((2, tall, tile_cols), f32),
            pltpu.VMEM((lines, columns, slot, tile_cols), f32),
            pltpu.SemaphoreType.DMA((1,)),
        ],
        out=HBM_SPEC,
    )(arrived)
    gathered = lax.all_to_all(
        parts.reshape(lines * columns, slot, tile_cols),
        ("line", "tile"),
        split_axis=0,
        concat_axis=0,
        tiled=True,
    )

    side = lax.axis_index("side").astype(jnp.int32).reshape(1, 1)
    strips, cross = call(
        gather_kernel,
        [
            jax.ShapeDtypeStruct((2 * lines, 2 * piece, tile_cols), f32),
            jax.ShapeDtypeStruct((4, tile_cols), f32),
        ],
        [SMEM_SPEC, VMEM_SPEC],
        (lines * columns * slot * tile_cols, 4 * lines * columns * slot * tile_cols),
    )(side, gathered)
    swap = [(i, i + 1) for i in range(1, rows - 1, 2)]
    cross = lax.ppermute(cross, ROW, swap + [(j, i) for i, j in swap])
    strips = lax.all_to_all(strips, ("line", "side"), split_axis=0, concat_axis=0, tiled=True)

    return call(
        finish_kernel,
        jax.ShapeDtypeStruct((tile_rows, tile_cols), f32),
        [SMEM_SPEC] + [VMEM_SPEC] * 3,
        (8 * tile_rows * tile_cols, 16 * tile_rows * tile_cols),
        [pltpu.VMEM((tile_rows, tile_cols), f32), pltpu.VMEM((tile_rows, tile_cols), f32)],
    )(side, strips, cross, prefire_elevation)


def solution(mesh):
    lines, columns, rows = (mesh.shape[a] for a in ("line", "tile", "row"))
    paired = Mesh(
        mesh.devices.reshape(lines, columns, rows // 2, 2), ("line", "tile", "pair", "side")
    )
    placed = (
        P(("line", "tile") + ROW, None),
        P(("line", "tile") + ROW, None),
        P(("line", "tile") + ROW, None),
        P(("line", "tile") + ROW),
        P("line", "tile", ROW),
        P(ROW, "tile"),
    )
    return jax.shard_map(
        per_device, mesh=paired, in_specs=placed, out_specs=P(ROW, "tile"), check_vma=False
    )
```

```python
import jax
import jax.numpy as jnp
from jax import lax
from jax.experimental import pallas as pl
from jax.experimental.pallas import tpu as pltpu
from jax.sharding import Mesh
from jax.sharding import PartitionSpec as P

VMEM_SPEC = pl.BlockSpec(memory_space=pltpu.VMEM)
HBM_SPEC = pl.BlockSpec(memory_space=pltpu.HBM)
SMEM_SPEC = pl.BlockSpec(memory_space=pltpu.SMEM)
PARAMS = pltpu.CompilerParams(vmem_limit_bytes=40 * 1024 * 1024)
WHOLE_PARAMS = pltpu.CompilerParams(vmem_limit_bytes=60 * 1024 * 1024)
CAPACITY = 2
ROW = ("pair", "side")
EVERY = ("line", "tile") + ROW
ROW_ORDER = [10, 0, 5, 11, 13, 6, 3, 14, 4, 12, 2, 9, 7, 15, 1, 8]
STRIP_ORDER = [27, 11, 0, 13, 29, 25, 31, 18, 17, 10, 5, 3, 4, 1, 15, 26, 12, 30, 21, 14, 2, 9, 28, 23, 8, 7, 16, 20, 24, 22, 19, 6]
END_ORDER = [0, 1, 2, 3, 4, 5, 6, 7]


def row_groups(lines, columns, rows):
    return [
        [(a * columns + b) * rows + z for z in ROW_ORDER]
        for a in range(lines)
        for b in range(columns)
    ]


def strip_groups(columns, rows):
    return [[m * rows + z for m in STRIP_ORDER] for z in range(rows)]


def end_groups(columns, rows):
    return [
        [(m // 2 * columns + b) * rows + 2 * p + m % 2 for m in END_ORDER]
        for b in range(columns)
        for p in range(rows // 2)
    ]


def call(kernel, out_shape, specs, cost, scratch=(), params=PARAMS):
    outs = jax.tree.map(lambda _: VMEM_SPEC, out_shape)
    return pl.pallas_call(
        kernel,
        out_shape=out_shape,
        in_specs=specs,
        out_specs=outs,
        scratch_shapes=list(scratch),
        compiler_params=params,
        cost_estimate=pl.CostEstimate(flops=cost[0], bytes_accessed=cost[1], transcendentals=0),
    )


def pack_kernel(rows, columns, tile_cols, *refs):
    _, dest_hbm, counts_ref, cells_hbm, heights_hbm, weights_hbm, out_ref = refs[:7]
    dest_ref, cells_ref, heights_ref, weights_ref, sems = refs[7:]
    copies = [
        pltpu.make_async_copy(source, target, sems.at[i])
        for i, (source, target) in enumerate(
            (
                (dest_hbm, dest_ref),
                (weights_hbm, weights_ref),
                (heights_hbm, heights_ref),
                (cells_hbm, cells_ref),
            )
        )
    ]
    for copy in copies:
        copy.start()
    copies[0].wait()
    blocks = cells_ref.shape[0]
    points = cells_ref.shape[1]
    here = columns * CAPACITY
    slots = rows * here
    dest = dest_ref[...]
    across = jnp.broadcast_to(dest.astype(jnp.float32), (blocks, blocks))
    down = across.T
    before = lax.broadcasted_iota(jnp.int32, (blocks, blocks), 0) < lax.broadcasted_iota(
        jnp.int32, (blocks, blocks), 1
    )
    same = jnp.where((across == down) & before, 1.0, 0.0)
    rank = jnp.sum(same, axis=0, keepdims=True).astype(jnp.int32)
    tile_row = dest % rows
    place = tile_row
    for position, row in enumerate(ROW_ORDER):
        place = jnp.where(tile_row == row, position, place)
    slot = place * here + (dest // rows) * CAPACITY + rank
    live = lax.broadcasted_iota(jnp.int32, (1, blocks), 1) < counts_ref[0, 0]
    slot = jnp.where(live, slot, slots)
    move = jnp.where(
        lax.broadcasted_iota(jnp.int32, (slots, blocks), 0) == slot, 1.0, 0.0
    ).astype(jnp.bfloat16)
    for copy in copies[1:]:
        copy.wait()
    weights = weights_ref[...]
    cells = cells_ref[...]
    payload = jnp.concatenate(
        [
            (weights * heights_ref[...]).astype(jnp.bfloat16),
            weights.astype(jnp.bfloat16),
            (cells // tile_cols).astype(jnp.float32).astype(jnp.bfloat16),
            (cells % tile_cols).astype(jnp.float32).astype(jnp.bfloat16),
        ],
        axis=1,
    )
    moved = jnp.dot(move, payload, preferred_element_type=jnp.float32)
    out_ref[:, 0:here, :] = moved[:, 0:points].reshape(rows, here, points)
    out_ref[:, here : 2 * here, :] = moved[:, points : 2 * points].reshape(rows, here, points)
    cell = moved[:, 2 * points : 3 * points] * tile_cols + moved[:, 3 * points :]
    out_ref[:, 2 * here :, :] = cell.reshape(rows, here, points)


def strip_kernel(lines, columns, tile_rows, tile_cols, in_ref, out_ref, *scratch):
    row_ref, col_ref, held_ref, near_ref, far_ref = scratch
    sources, held, points = in_ref.shape
    here = held // 3
    piece = tile_rows // lines
    tall = tile_rows + 16
    first, end = 8, 8 + tile_rows
    cells = in_ref[:, 2 * here :, :].astype(jnp.int32)
    row_ref[...] = (cells // tile_cols).astype(jnp.float32)
    col_ref[...] = (cells % tile_cols).astype(jnp.float32)
    row_ids = lax.broadcasted_iota(jnp.int32, (tile_rows, points), 0)
    row_ids = row_ids.astype(jnp.float32).astype(jnp.bfloat16)
    col_ids = lax.broadcasted_iota(jnp.int32, (tile_cols, points), 0)
    col_ids = col_ids.astype(jnp.float32).astype(jnp.bfloat16)
    zero = jnp.zeros((tile_rows, points), jnp.bfloat16)
    one_col = jnp.ones((tile_cols, points), jnp.bfloat16)
    zero_col = jnp.zeros((tile_cols, points), jnp.bfloat16)
    lane = lax.broadcasted_iota(jnp.int32, (tall, tile_cols), 1)
    blank = jnp.zeros((tall, tile_cols), jnp.float32)
    margin = jnp.zeros((8, tile_cols), jnp.float32)

    def spread(ref, source, at, count):
        line = ref[source, pl.ds(at, 1), :]
        return jnp.broadcast_to(line, (count, points)).astype(jnp.bfloat16)

    def add_up(column):
        total = jnp.zeros((2 * tile_rows, tile_cols), jnp.float32)
        for source in range(0, sources, 2):
            lefts, rights = [], []
            for s in (source, source + 1):
                for k in range(CAPACITY):
                    at = column * CAPACITY + k
                    hit = spread(row_ref, s, at, tile_rows) == row_ids
                    wz = spread(in_ref, s, at, tile_rows)
                    w = spread(in_ref, s, here + at, tile_rows)
                    lefts.append(
                        jnp.concatenate([jnp.where(hit, wz, zero), jnp.where(hit, w, zero)], axis=0)
                    )
                    rights.append(
                        jnp.where(spread(col_ref, s, at, tile_cols) == col_ids, one_col, zero_col)
                    )
            total = total + lax.dot_general(
                jnp.concatenate(lefts, axis=1),
                jnp.concatenate(rights, axis=1),
                (((1,), (1,)), ((), ())),
                preferred_element_type=jnp.float32,
            )
        for value in range(2):
            held_ref[value, column, 0:first, :] = margin
            held_ref[value, column, first:end, :] = total[
                value * tile_rows : (value + 1) * tile_rows, :
            ]
            held_ref[value, column, end:, :] = margin

    def turned(value, column):
        if column < 0 or column >= columns:
            return blank, blank, blank, blank
        x = held_ref[value, column]
        return tuple(pltpu.roll(x, s, 1) for s in (1, 2, tile_cols - 1, tile_cols - 2))

    def filter_column(value, column, before, here, after):
        x = held_ref[value, column]
        one = jnp.where(lane < 1, before[0], here[0]) + jnp.where(
            lane >= tile_cols - 1, after[2], here[2]
        )
        two = jnp.where(lane < 2, before[1], here[1]) + jnp.where(
            lane >= tile_cols - 2, after[3], here[3]
        )
        same = 2.0 * x + one + 0.25 * two
        near_ref[value] = x + 0.5 * one + 0.2 * two
        far_ref[value] = 0.25 * x + 0.2 * one + 0.125 * two

        def near(at, count):
            return near_ref[value, at : at + count, :]

        def far(at, count):
            return far_ref[value, at : at + count, :]

        inner = (
            same[first:end, :]
            + near(first - 1, tile_rows)
            + near(first + 1, tile_rows)
            + far(first - 2, tile_rows)
            + far(first + 2, tile_rows)
        )
        outer = jnp.concatenate(
            [
                far(first, 1),
                near(first, 1) + far(first + 1, 1),
                near(end - 1, 1) + far(end - 2, 1),
                far(end - 1, 1),
            ],
            axis=0,
        )
        base = 2 * piece + 2 * value
        for line in range(lines):
            at = STRIP_ORDER.index(line * columns + column)
            out_ref[at, value * piece : (value + 1) * piece, :] = inner[
                line * piece : (line + 1) * piece, :
            ]
            out_ref[at, base : base + 2, :] = outer[0:2]
            out_ref[at, base + 4 : base + 6, :] = outer[2:4]

    add_up(0)
    before = [turned(value, -1) for value in range(2)]
    here_now = [turned(value, 0) for value in range(2)]
    for column in range(columns):
        if column + 1 < columns:
            add_up(column + 1)
        after = [turned(value, column + 1) for value in range(2)]
        for value in range(2):
            filter_column(value, column, before[value], here_now[value], after[value])
        before, here_now = here_now, after


def end_places(line, side):
    lower, upper = END_ORDER.index(2 * line), END_ORDER.index(2 * line + 1)
    return jnp.where(side == 0, lower, upper), jnp.where(side == 0, upper, lower)


def gather_kernel(side_ref, parts_ref, strips_ref, cross_ref):
    sources = parts_ref.shape[0]
    ends, both, tile_cols = strips_ref.shape
    total = parts_ref[0]
    for source in range(1, sources):
        total = total + parts_ref[source]
    above = total[both : both + 4]
    below = total[both + 4 :]
    side = side_ref[0, 0]
    lower = side == 0
    partner = jnp.concatenate(
        [jnp.where(lower, below, above), jnp.zeros((both - 4, tile_cols), jnp.float32)], axis=0
    )
    for line in range(ends // 2):
        here, there = end_places(line, side)
        strips_ref[here] = total[:both]
        strips_ref[there] = partner
    cross_ref[...] = jnp.where(lower, above, below)


def finish_kernel(side_ref, strips_ref, cross_ref, prefire_ref, out_ref, wz_ref, w_ref):
    ends, both, _ = strips_ref.shape
    lines = ends // 2
    piece = both // 2
    rows = lines * piece
    side = side_ref[0, 0]
    partner = strips_ref[end_places(0, side)[1], 0:4, :]
    cross = cross_ref[...]
    top = jnp.where(side == 0, cross, partner)
    bottom = jnp.where(side == 0, partner, cross)
    for value, ref in enumerate((wz_ref, w_ref)):
        for line in range(lines):
            ref[line * piece : (line + 1) * piece, :] = strips_ref[
                end_places(line, side)[0], value * piece : (value + 1) * piece, :
            ]
        ref[0:2, :] = ref[0:2, :] + top[2 * value : 2 * value + 2]
        ref[rows - 2 :, :] = ref[rows - 2 :, :] + bottom[2 * value : 2 * value + 2]
    prefire = prefire_ref[...]
    filled = (wz_ref[...] + 16.0 * prefire) / (w_ref[...] + 16.0)
    out_ref[...] = filled - prefire


def per_device(cells, heights, weights, dest, counts, prefire_elevation):
    lines, columns, rows = (lax.axis_size(a) for a in ("line", "tile", ROW))
    blocks, points = cells.shape
    tile_rows, tile_cols = prefire_elevation.shape
    here = columns * CAPACITY
    f32 = jnp.float32
    piece = tile_rows // lines

    side = lax.axis_index("side").astype(jnp.int32).reshape(1, 1)
    packed = call(
        lambda *refs: pack_kernel(rows, columns, tile_cols, *refs),
        jax.ShapeDtypeStruct((rows, 3 * here, points), f32),
        [SMEM_SPEC, HBM_SPEC, SMEM_SPEC, HBM_SPEC, HBM_SPEC, HBM_SPEC],
        (2 * rows * here * blocks * 4 * points, 4 * 6 * rows * here * points),
        [
            pltpu.VMEM((1, blocks), jnp.int32),
            pltpu.VMEM((blocks, points), jnp.int32),
            pltpu.VMEM((blocks, points), f32),
            pltpu.VMEM((blocks, points), f32),
            pltpu.SemaphoreType.DMA((4,)),
        ],
        params=WHOLE_PARAMS,
    )(side, dest.reshape(1, blocks), counts.reshape(1, 1), cells, heights, weights)
    arrived = lax.all_to_all(
        packed,
        EVERY,
        split_axis=0,
        concat_axis=0,
        tiled=True,
        axis_index_groups=row_groups(lines, columns, rows),
    )

    tall = tile_rows + 16
    slot = 2 * piece + 8
    parts = call(
        lambda *refs: strip_kernel(lines, columns, tile_rows, tile_cols, *refs),
        jax.ShapeDtypeStruct((lines * columns, slot, tile_cols), f32),
        [VMEM_SPEC],
        (4 * rows * here * points * tile_rows * tile_cols, 4 * 4 * rows * here * points),
        [
            pltpu.VMEM((rows, here, points), f32),
            pltpu.VMEM((rows, here, points), f32),
            pltpu.VMEM((2, columns, tall, tile_cols), f32),
            pltpu.VMEM((2, tall, tile_cols), f32),
            pltpu.VMEM((2, tall, tile_cols), f32),
        ],
    )(arrived)
    gathered = lax.all_to_all(
        parts,
        EVERY,
        split_axis=0,
        concat_axis=0,
        tiled=True,
        axis_index_groups=strip_groups(columns, rows),
    )

    strips, cross = call(
        gather_kernel,
        [
            jax.ShapeDtypeStruct((2 * lines, 2 * piece, tile_cols), f32),
            jax.ShapeDtypeStruct((4, tile_cols), f32),
        ],
        [SMEM_SPEC, VMEM_SPEC],
        (lines * columns * slot * tile_cols, 4 * lines * columns * slot * tile_cols),
    )(side, gathered)
    swap = [(i, i + 1) for i in range(1, rows - 1, 2)]
    cross = lax.ppermute(cross, ROW, swap + [(j, i) for i, j in swap])
    strips = lax.all_to_all(
        strips,
        EVERY,
        split_axis=0,
        concat_axis=0,
        tiled=True,
        axis_index_groups=end_groups(columns, rows),
    )

    return call(
        finish_kernel,
        jax.ShapeDtypeStruct((tile_rows, tile_cols), f32),
        [SMEM_SPEC] + [VMEM_SPEC] * 3,
        (8 * tile_rows * tile_cols, 16 * tile_rows * tile_cols),
        [pltpu.VMEM((tile_rows, tile_cols), f32), pltpu.VMEM((tile_rows, tile_cols), f32)],
    )(side, strips, cross, prefire_elevation)


def solution(mesh):
    lines, columns, rows = (mesh.shape[a] for a in ("line", "tile", "row"))
    paired = Mesh(
        mesh.devices.reshape(lines, columns, rows // 2, 2), ("line", "tile", "pair", "side")
    )
    placed = (
        P(("line", "tile") + ROW, None),
        P(("line", "tile") + ROW, None),
        P(("line", "tile") + ROW, None),
        P(("line", "tile") + ROW),
        P("line", "tile", ROW),
        P(ROW, "tile"),
    )
    return jax.shard_map(
        per_device, mesh=paired, in_specs=placed, out_specs=P(ROW, "tile"), check_vma=False
    )
```

```python
import jax
import jax.numpy as jnp
from jax import lax
from jax.experimental import pallas as pl
from jax.experimental.pallas import tpu as pltpu
from jax.sharding import Mesh
from jax.sharding import PartitionSpec as P

VMEM_SPEC = pl.BlockSpec(memory_space=pltpu.VMEM)
HBM_SPEC = pl.BlockSpec(memory_space=pltpu.HBM)
SMEM_SPEC = pl.BlockSpec(memory_space=pltpu.SMEM)
PARAMS = pltpu.CompilerParams(vmem_limit_bytes=40 * 1024 * 1024)
WHOLE_PARAMS = pltpu.CompilerParams(vmem_limit_bytes=60 * 1024 * 1024)
CAPACITY = 2
ROW = ("pair", "side")
EVERY = ("line", "tile") + ROW
ROW_ORDER = [10, 0, 5, 11, 13, 6, 3, 14, 4, 12, 2, 9, 7, 15, 1, 8]
STRIP_ORDER = [27, 28, 29, 30, 31, 0, 1, 2, 3, 4, 5, 6, 7, 8, 9, 10, 11, 12, 13, 14, 15, 16, 17, 18, 19, 20, 21, 22, 23, 24, 25, 26]
END_ORDER = [0, 1, 2, 3, 4, 5, 6, 7]


def row_groups(lines, columns, rows):
    return [
        [(a * columns + b) * rows + z for z in ROW_ORDER]
        for a in range(lines)
        for b in range(columns)
    ]


def strip_groups(columns, rows):
    return [[m * rows + z for m in STRIP_ORDER] for z in range(rows)]


def end_groups(columns, rows):
    return [
        [(m // 2 * columns + b) * rows + 2 * p + m % 2 for m in END_ORDER]
        for b in range(columns)
        for p in range(rows // 2)
    ]


def call(kernel, out_shape, specs, cost, scratch=(), params=PARAMS):
    outs = jax.tree.map(lambda _: VMEM_SPEC, out_shape)
    return pl.pallas_call(
        kernel,
        out_shape=out_shape,
        in_specs=specs,
        out_specs=outs,
        scratch_shapes=list(scratch),
        compiler_params=params,
        cost_estimate=pl.CostEstimate(flops=cost[0], bytes_accessed=cost[1], transcendentals=0),
    )


def pack_kernel(rows, columns, tile_cols, *refs):
    _, dest_hbm, counts_ref, cells_hbm, heights_hbm, weights_hbm, out_ref = refs[:7]
    dest_ref, cells_ref, heights_ref, weights_ref, sems = refs[7:]
    copies = [
        pltpu.make_async_copy(source, target, sems.at[i])
        for i, (source, target) in enumerate(
            (
                (dest_hbm, dest_ref),
                (weights_hbm, weights_ref),
                (heights_hbm, heights_ref),
                (cells_hbm, cells_ref),
            )
        )
    ]
    for copy in copies:
        copy.start()
    copies[0].wait()
    blocks = cells_ref.shape[0]
    points = cells_ref.shape[1]
    here = columns * CAPACITY
    slots = rows * here
    dest = dest_ref[...]
    across = jnp.broadcast_to(dest.astype(jnp.float32), (blocks, blocks))
    down = across.T
    before = lax.broadcasted_iota(jnp.int32, (blocks, blocks), 0) < lax.broadcasted_iota(
        jnp.int32, (blocks, blocks), 1
    )
    same = jnp.where((across == down) & before, 1.0, 0.0)
    rank = jnp.sum(same, axis=0, keepdims=True).astype(jnp.int32)
    tile_row = dest % rows
    place = tile_row
    for position, row in enumerate(ROW_ORDER):
        place = jnp.where(tile_row == row, position, place)
    slot = place * here + (dest // rows) * CAPACITY + rank
    live = lax.broadcasted_iota(jnp.int32, (1, blocks), 1) < counts_ref[0, 0]
    slot = jnp.where(live, slot, slots)
    move = jnp.where(
        lax.broadcasted_iota(jnp.int32, (slots, blocks), 0) == slot, 1.0, 0.0
    ).astype(jnp.bfloat16)
    for copy in copies[1:]:
        copy.wait()
    weights = weights_ref[...]
    cells = cells_ref[...]
    payload = jnp.concatenate(
        [
            (weights * heights_ref[...]).astype(jnp.bfloat16),
            weights.astype(jnp.bfloat16),
            (cells // tile_cols).astype(jnp.float32).astype(jnp.bfloat16),
            (cells % tile_cols).astype(jnp.float32).astype(jnp.bfloat16),
        ],
        axis=1,
    )
    moved = jnp.dot(move, payload, preferred_element_type=jnp.float32)
    out_ref[:, 0:here, :] = moved[:, 0:points].reshape(rows, here, points)
    out_ref[:, here : 2 * here, :] = moved[:, points : 2 * points].reshape(rows, here, points)
    cell = moved[:, 2 * points : 3 * points] * tile_cols + moved[:, 3 * points :]
    out_ref[:, 2 * here :, :] = cell.reshape(rows, here, points)


def strip_kernel(lines, columns, tile_rows, tile_cols, in_ref, out_ref, *scratch):
    row_ref, col_ref, held_ref, near_ref, far_ref = scratch
    sources, held, points = in_ref.shape
    here = held // 3
    piece = tile_rows // lines
    tall = tile_rows + 16
    first, end = 8, 8 + tile_rows
    cells = in_ref[:, 2 * here :, :].astype(jnp.int32)
    row_ref[...] = (cells // tile_cols).astype(jnp.float32)
    col_ref[...] = (cells % tile_cols).astype(jnp.float32)
    row_ids = lax.broadcasted_iota(jnp.int32, (tile_rows, points), 0)
    row_ids = row_ids.astype(jnp.float32).astype(jnp.bfloat16)
    col_ids = lax.broadcasted_iota(jnp.int32, (tile_cols, points), 0)
    col_ids = col_ids.astype(jnp.float32).astype(jnp.bfloat16)
    zero = jnp.zeros((tile_rows, points), jnp.bfloat16)
    one_col = jnp.ones((tile_cols, points), jnp.bfloat16)
    zero_col = jnp.zeros((tile_cols, points), jnp.bfloat16)
    lane = lax.broadcasted_iota(jnp.int32, (tall, tile_cols), 1)
    blank = jnp.zeros((tall, tile_cols), jnp.float32)
    margin = jnp.zeros((8, tile_cols), jnp.float32)

    def spread(ref, source, at, count):
        line = ref[source, pl.ds(at, 1), :]
        return jnp.broadcast_to(line, (count, points)).astype(jnp.bfloat16)

    def add_up(column):
        total = jnp.zeros((2 * tile_rows, tile_cols), jnp.float32)
        for source in range(0, sources, 2):
            lefts, rights = [], []
            for s in (source, source + 1):
                for k in range(CAPACITY):
                    at = column * CAPACITY + k
                    hit = spread(row_ref, s, at, tile_rows) == row_ids
                    wz = spread(in_ref, s, at, tile_rows)
                    w = spread(in_ref, s, here + at, tile_rows)
                    lefts.append(
                        jnp.concatenate([jnp.where(hit, wz, zero), jnp.where(hit, w, zero)], axis=0)
                    )
                    rights.append(
                        jnp.where(spread(col_ref, s, at, tile_cols) == col_ids, one_col, zero_col)
                    )
            total = total + lax.dot_general(
                jnp.concatenate(lefts, axis=1),
                jnp.concatenate(rights, axis=1),
                (((1,), (1,)), ((), ())),
                preferred_element_type=jnp.float32,
            )
        for value in range(2):
            held_ref[value, column, 0:first, :] = margin
            held_ref[value, column, first:end, :] = total[
                value * tile_rows : (value + 1) * tile_rows, :
            ]
            held_ref[value, column, end:, :] = margin

    def turned(value, column):
        if column < 0 or column >= columns:
            return blank, blank, blank, blank
        x = held_ref[value, column]
        return tuple(pltpu.roll(x, s, 1) for s in (1, 2, tile_cols - 1, tile_cols - 2))

    def filter_column(value, column, before, here, after):
        x = held_ref[value, column]
        one = jnp.where(lane < 1, before[0], here[0]) + jnp.where(
            lane >= tile_cols - 1, after[2], here[2]
        )
        two = jnp.where(lane < 2, before[1], here[1]) + jnp.where(
            lane >= tile_cols - 2, after[3], here[3]
        )
        same = 2.0 * x + one + 0.25 * two
        near_ref[value] = x + 0.5 * one + 0.2 * two
        far_ref[value] = 0.25 * x + 0.2 * one + 0.125 * two

        def near(at, count):
            return near_ref[value, at : at + count, :]

        def far(at, count):
            return far_ref[value, at : at + count, :]

        inner = (
            same[first:end, :]
            + near(first - 1, tile_rows)
            + near(first + 1, tile_rows)
            + far(first - 2, tile_rows)
            + far(first + 2, tile_rows)
        )
        outer = jnp.concatenate(
            [
                far(first, 1),
                near(first, 1) + far(first + 1, 1),
                near(end - 1, 1) + far(end - 2, 1),
                far(end - 1, 1),
            ],
            axis=0,
        )
        base = 2 * piece + 2 * value
        for line in range(lines):
            at = STRIP_ORDER.index(line * columns + column)
            out_ref[at, value * piece : (value + 1) * piece, :] = inner[
                line * piece : (line + 1) * piece, :
            ]
            out_ref[at, base : base + 2, :] = outer[0:2]
            out_ref[at, base + 4 : base + 6, :] = outer[2:4]

    add_up(0)
    before = [turned(value, -1) for value in range(2)]
    here_now = [turned(value, 0) for value in range(2)]
    for column in range(columns):
        if column + 1 < columns:
            add_up(column + 1)
        after = [turned(value, column + 1) for value in range(2)]
        for value in range(2):
            filter_column(value, column, before[value], here_now[value], after[value])
        before, here_now = here_now, after


def end_places(line, side):
    lower, upper = END_ORDER.index(2 * line), END_ORDER.index(2 * line + 1)
    return jnp.where(side == 0, lower, upper), jnp.where(side == 0, upper, lower)


def gather_kernel(side_ref, parts_ref, strips_ref, cross_ref):
    sources = parts_ref.shape[0]
    ends, both, tile_cols = strips_ref.shape
    total = parts_ref[0]
    for source in range(1, sources):
        total = total + parts_ref[source]
    above = total[both : both + 4]
    below = total[both + 4 :]
    side = side_ref[0, 0]
    lower = side == 0
    partner = jnp.concatenate(
        [jnp.where(lower, below, above), jnp.zeros((both - 4, tile_cols), jnp.float32)], axis=0
    )
    for line in range(ends // 2):
        here, there = end_places(line, side)
        strips_ref[here] = total[:both]
        strips_ref[there] = partner
    cross_ref[...] = jnp.where(lower, above, below)


def finish_kernel(side_ref, strips_ref, cross_ref, prefire_ref, out_ref, wz_ref, w_ref):
    ends, both, _ = strips_ref.shape
    lines = ends // 2
    piece = both // 2
    rows = lines * piece
    side = side_ref[0, 0]
    partner = strips_ref[end_places(0, side)[1], 0:4, :]
    cross = cross_ref[...]
    top = jnp.where(side == 0, cross, partner)
    bottom = jnp.where(side == 0, partner, cross)
    for value, ref in enumerate((wz_ref, w_ref)):
        for line in range(lines):
            ref[line * piece : (line + 1) * piece, :] = strips_ref[
                end_places(line, side)[0], value * piece : (value + 1) * piece, :
            ]
        ref[0:2, :] = ref[0:2, :] + top[2 * value : 2 * value + 2]
        ref[rows - 2 :, :] = ref[rows - 2 :, :] + bottom[2 * value : 2 * value + 2]
    prefire = prefire_ref[...]
    filled = (wz_ref[...] + 16.0 * prefire) / (w_ref[...] + 16.0)
    out_ref[...] = filled - prefire


def per_device(cells, heights, weights, dest, counts, prefire_elevation):
    lines, columns, rows = (lax.axis_size(a) for a in ("line", "tile", ROW))
    blocks, points = cells.shape
    tile_rows, tile_cols = prefire_elevation.shape
    here = columns * CAPACITY
    f32 = jnp.float32
    piece = tile_rows // lines

    side = lax.axis_index("side").astype(jnp.int32).reshape(1, 1)
    packed = call(
        lambda *refs: pack_kernel(rows, columns, tile_cols, *refs),
        jax.ShapeDtypeStruct((rows, 3 * here, points), f32),
        [SMEM_SPEC, HBM_SPEC, SMEM_SPEC, HBM_SPEC, HBM_SPEC, HBM_SPEC],
        (2 * rows * here * blocks * 4 * points, 4 * 6 * rows * here * points),
        [
            pltpu.VMEM((1, blocks), jnp.int32),
            pltpu.VMEM((blocks, points), jnp.int32),
            pltpu.VMEM((blocks, points), f32),
            pltpu.VMEM((blocks, points), f32),
            pltpu.SemaphoreType.DMA((4,)),
        ],
        params=WHOLE_PARAMS,
    )(side, dest.reshape(1, blocks), counts.reshape(1, 1), cells, heights, weights)
    arrived = lax.all_to_all(
        packed,
        EVERY,
        split_axis=0,
        concat_axis=0,
        tiled=True,
        axis_index_groups=row_groups(lines, columns, rows),
    )

    tall = tile_rows + 16
    slot = 2 * piece + 8
    parts = call(
        lambda *refs: strip_kernel(lines, columns, tile_rows, tile_cols, *refs),
        jax.ShapeDtypeStruct((lines * columns, slot, tile_cols), f32),
        [VMEM_SPEC],
        (4 * rows * here * points * tile_rows * tile_cols, 4 * 4 * rows * here * points),
        [
            pltpu.VMEM((rows, here, points), f32),
            pltpu.VMEM((rows, here, points), f32),
            pltpu.VMEM((2, columns, tall, tile_cols), f32),
            pltpu.VMEM((2, tall, tile_cols), f32),
            pltpu.VMEM((2, tall, tile_cols), f32),
        ],
    )(arrived)
    gathered = lax.all_to_all(
        parts,
        EVERY,
        split_axis=0,
        concat_axis=0,
        tiled=True,
        axis_index_groups=strip_groups(columns, rows),
    )

    strips, cross = call(
        gather_kernel,
        [
            jax.ShapeDtypeStruct((2 * lines, 2 * piece, tile_cols), f32),
            jax.ShapeDtypeStruct((4, tile_cols), f32),
        ],
        [SMEM_SPEC, VMEM_SPEC],
        (lines * columns * slot * tile_cols, 4 * lines * columns * slot * tile_cols),
    )(side, gathered)
    swap = [(i, i + 1) for i in range(1, rows - 1, 2)]
    cross = lax.ppermute(cross, ROW, swap + [(j, i) for i, j in swap])
    strips = lax.all_to_all(
        strips,
        EVERY,
        split_axis=0,
        concat_axis=0,
        tiled=True,
        axis_index_groups=end_groups(columns, rows),
    )

    return call(
        finish_kernel,
        jax.ShapeDtypeStruct((tile_rows, tile_cols), f32),
        [SMEM_SPEC] + [VMEM_SPEC] * 3,
        (8 * tile_rows * tile_cols, 16 * tile_rows * tile_cols),
        [pltpu.VMEM((tile_rows, tile_cols), f32), pltpu.VMEM((tile_rows, tile_cols), f32)],
    )(side, strips, cross, prefire_elevation)


def solution(mesh):
    lines, columns, rows = (mesh.shape[a] for a in ("line", "tile", "row"))
    paired = Mesh(
        mesh.devices.reshape(lines, columns, rows // 2, 2), ("line", "tile", "pair", "side")
    )
    placed = (
        P(("line", "tile") + ROW, None),
        P(("line", "tile") + ROW, None),
        P(("line", "tile") + ROW, None),
        P(("line", "tile") + ROW),
        P("line", "tile", ROW),
        P(ROW, "tile"),
    )
    return jax.shard_map(
        per_device, mesh=paired, in_specs=placed, out_specs=P(ROW, "tile"), check_vma=False
    )
```

```python
import jax
import jax.numpy as jnp
from jax import lax
from jax.experimental import pallas as pl
from jax.experimental.pallas import tpu as pltpu
from jax.sharding import Mesh
from jax.sharding import PartitionSpec as P

VMEM_SPEC = pl.BlockSpec(memory_space=pltpu.VMEM)
HBM_SPEC = pl.BlockSpec(memory_space=pltpu.HBM)
SMEM_SPEC = pl.BlockSpec(memory_space=pltpu.SMEM)
PARAMS = pltpu.CompilerParams(vmem_limit_bytes=40 * 1024 * 1024)
WHOLE_PARAMS = pltpu.CompilerParams(vmem_limit_bytes=60 * 1024 * 1024)
CAPACITY = 2
ROW = ("pair", "side")
EVERY = ("line", "tile") + ROW
ROW_ORDER = [10, 0, 5, 11, 13, 6, 3, 14, 4, 12, 2, 9, 7, 15, 1, 8]
STRIP_ORDER = [27, 28, 29, 30, 31, 0, 1, 2, 3, 4, 5, 6, 7, 8, 9, 10, 11, 12, 13, 14, 15, 16, 17, 18, 19, 20, 21, 22, 23, 24, 25, 26]
END_ORDER = [0, 1, 2, 3, 4, 5, 6, 7]


def row_groups(lines, columns, rows):
    return [
        [(a * columns + b) * rows + z for z in ROW_ORDER]
        for a in range(lines)
        for b in range(columns)
    ]


def strip_groups(columns, rows):
    return [[m * rows + z for m in STRIP_ORDER] for z in range(rows)]


def end_groups(columns, rows):
    return [
        [(m // 2 * columns + b) * rows + 2 * p + m % 2 for m in END_ORDER]
        for b in range(columns)
        for p in range(rows // 2)
    ]


def call(kernel, out_shape, specs, cost, scratch=(), params=PARAMS):
    outs = jax.tree.map(lambda _: VMEM_SPEC, out_shape)
    return pl.pallas_call(
        kernel,
        out_shape=out_shape,
        in_specs=specs,
        out_specs=outs,
        scratch_shapes=list(scratch),
        compiler_params=params,
        cost_estimate=pl.CostEstimate(flops=cost[0], bytes_accessed=cost[1], transcendentals=0),
    )


def pack_kernel(rows, columns, tile_cols, *refs):
    _, dest_hbm, counts_ref, cells_hbm, heights_hbm, weights_hbm, out_ref = refs[:7]
    dest_ref, cells_ref, heights_ref, weights_ref, sems = refs[7:]
    copies = [
        pltpu.make_async_copy(source, target, sems.at[i])
        for i, (source, target) in enumerate(
            (
                (dest_hbm, dest_ref),
                (weights_hbm, weights_ref),
                (heights_hbm, heights_ref),
                (cells_hbm, cells_ref),
            )
        )
    ]
    for copy in copies:
        copy.start()
    copies[0].wait()
    blocks = cells_ref.shape[0]
    points = cells_ref.shape[1]
    here = columns * CAPACITY
    slots = rows * here
    dest = dest_ref[...]
    across = jnp.broadcast_to(dest.astype(jnp.float32), (blocks, blocks))
    down = across.T
    before = lax.broadcasted_iota(jnp.int32, (blocks, blocks), 0) < lax.broadcasted_iota(
        jnp.int32, (blocks, blocks), 1
    )
    same = jnp.where((across == down) & before, 1.0, 0.0)
    rank = jnp.sum(same, axis=0, keepdims=True).astype(jnp.int32)
    tile_row = dest % rows
    place = tile_row
    for position, row in enumerate(ROW_ORDER):
        place = jnp.where(tile_row == row, position, place)
    slot = place * here + (dest // rows) * CAPACITY + rank
    live = lax.broadcasted_iota(jnp.int32, (1, blocks), 1) < counts_ref[0, 0]
    slot = jnp.where(live, slot, slots)
    move = jnp.where(
        lax.broadcasted_iota(jnp.int32, (slots, blocks), 0) == slot, 1.0, 0.0
    ).astype(jnp.bfloat16)
    for copy in copies[1:]:
        copy.wait()
    weights = weights_ref[...]
    cells = cells_ref[...]
    payload = jnp.concatenate(
        [
            (weights * heights_ref[...]).astype(jnp.bfloat16),
            weights.astype(jnp.bfloat16),
            (cells // tile_cols).astype(jnp.float32).astype(jnp.bfloat16),
            (cells % tile_cols).astype(jnp.float32).astype(jnp.bfloat16),
        ],
        axis=1,
    )
    moved = jnp.dot(move, payload, preferred_element_type=jnp.float32)
    out_ref[:, 0:here, :] = moved[:, 0:points].reshape(rows, here, points)
    out_ref[:, here : 2 * here, :] = moved[:, points : 2 * points].reshape(rows, here, points)
    cell = moved[:, 2 * points : 3 * points] * tile_cols + moved[:, 3 * points :]
    out_ref[:, 2 * here :, :] = cell.reshape(rows, here, points)


def strip_kernel(lines, columns, tile_rows, tile_cols, in_ref, out_ref, *scratch):
    row_ref, col_ref, held_ref, near_ref, far_ref = scratch
    sources, held, points = in_ref.shape
    here = held // 3
    piece = tile_rows // lines
    first, end = 8, 8 + tile_rows
    cells = in_ref[:, 2 * here :, :].astype(jnp.int32)
    row_ref[...] = (cells // tile_cols).astype(jnp.float32)
    col_ref[...] = (cells % tile_cols).astype(jnp.float32)
    row_ids = lax.broadcasted_iota(jnp.int32, (tile_rows, points), 0)
    row_ids = row_ids.astype(jnp.float32).astype(jnp.bfloat16)
    col_ids = lax.broadcasted_iota(jnp.int32, (tile_cols, points), 0)
    col_ids = col_ids.astype(jnp.float32).astype(jnp.bfloat16)
    zero = jnp.zeros((tile_rows, points), jnp.bfloat16)
    one_col = jnp.ones((tile_cols, points), jnp.bfloat16)
    zero_col = jnp.zeros((tile_cols, points), jnp.bfloat16)
    lane = lax.broadcasted_iota(jnp.int32, (tile_rows, tile_cols), 1)
    blank = jnp.zeros((tile_rows, tile_cols), jnp.float32)
    margin = jnp.zeros((2, 8, tile_cols), jnp.float32)
    for ref in (near_ref, far_ref):
        ref[:, 0:first, :] = margin
        ref[:, end:, :] = margin

    def spread(ref, source, at, count):
        line = ref[source, pl.ds(at, 1), :]
        return jnp.broadcast_to(line, (count, points)).astype(jnp.bfloat16)

    def add_up(column):
        total = jnp.zeros((2 * tile_rows, tile_cols), jnp.float32)
        for source in range(0, sources, 2):
            lefts, rights = [], []
            for s in (source, source + 1):
                for k in range(CAPACITY):
                    at = column * CAPACITY + k
                    hit = spread(row_ref, s, at, tile_rows) == row_ids
                    wz = spread(in_ref, s, at, tile_rows)
                    w = spread(in_ref, s, here + at, tile_rows)
                    lefts.append(
                        jnp.concatenate([jnp.where(hit, wz, zero), jnp.where(hit, w, zero)], axis=0)
                    )
                    rights.append(
                        jnp.where(spread(col_ref, s, at, tile_cols) == col_ids, one_col, zero_col)
                    )
            total = total + lax.dot_general(
                jnp.concatenate(lefts, axis=1),
                jnp.concatenate(rights, axis=1),
                (((1,), (1,)), ((), ())),
                preferred_element_type=jnp.float32,
            )
        for value in range(2):
            held_ref[value, column] = total[value * tile_rows : (value + 1) * tile_rows, :]

    def turned(value, column):
        if column < 0 or column >= columns:
            return blank, blank, blank, blank
        x = held_ref[value, column]
        return tuple(pltpu.roll(x, s, 1) for s in (1, 2, tile_cols - 1, tile_cols - 2))

    def filter_column(value, column, before, here, after):
        x = held_ref[value, column]
        one = jnp.where(lane < 1, before[0], here[0]) + jnp.where(
            lane >= tile_cols - 1, after[2], here[2]
        )
        two = jnp.where(lane < 2, before[1], here[1]) + jnp.where(
            lane >= tile_cols - 2, after[3], here[3]
        )
        same = 2.0 * x + one + 0.25 * two
        near_ref[value, first:end, :] = x + 0.5 * one + 0.2 * two
        far_ref[value, first:end, :] = 0.25 * x + 0.2 * one + 0.125 * two

        def near(at, count):
            return near_ref[value, at : at + count, :]

        def far(at, count):
            return far_ref[value, at : at + count, :]

        inner = (
            same
            + near(first - 1, tile_rows)
            + near(first + 1, tile_rows)
            + far(first - 2, tile_rows)
            + far(first + 2, tile_rows)
        )
        outer = jnp.concatenate(
            [
                far(first, 1),
                near(first, 1) + far(first + 1, 1),
                near(end - 1, 1) + far(end - 2, 1),
                far(end - 1, 1),
            ],
            axis=0,
        )
        base = 2 * piece + 2 * value
        for line in range(lines):
            at = STRIP_ORDER.index(line * columns + column)
            out_ref[at, value * piece : (value + 1) * piece, :] = inner[
                line * piece : (line + 1) * piece, :
            ]
            out_ref[at, base : base + 2, :] = outer[0:2]
            out_ref[at, base + 4 : base + 6, :] = outer[2:4]

    add_up(0)
    before = [turned(value, -1) for value in range(2)]
    here_now = [turned(value, 0) for value in range(2)]
    for column in range(columns):
        if column + 1 < columns:
            add_up(column + 1)
        after = [turned(value, column + 1) for value in range(2)]
        for value in range(2):
            filter_column(value, column, before[value], here_now[value], after[value])
        before, here_now = here_now, after


def end_places(line, side):
    lower, upper = END_ORDER.index(2 * line), END_ORDER.index(2 * line + 1)
    return jnp.where(side == 0, lower, upper), jnp.where(side == 0, upper, lower)


def gather_kernel(side_ref, parts_ref, strips_ref, cross_ref):
    sources = parts_ref.shape[0]
    ends, both, tile_cols = strips_ref.shape
    total = parts_ref[0]
    for source in range(1, sources):
        total = total + parts_ref[source]
    above = total[both : both + 4]
    below = total[both + 4 :]
    side = side_ref[0, 0]
    lower = side == 0
    partner = jnp.concatenate(
        [jnp.where(lower, below, above), jnp.zeros((both - 4, tile_cols), jnp.float32)], axis=0
    )
    for line in range(ends // 2):
        here, there = end_places(line, side)
        strips_ref[here] = total[:both]
        strips_ref[there] = partner
    cross_ref[...] = jnp.where(lower, above, below)


def finish_kernel(side_ref, strips_ref, cross_ref, prefire_ref, out_ref, wz_ref, w_ref):
    ends, both, _ = strips_ref.shape
    lines = ends // 2
    piece = both // 2
    rows = lines * piece
    side = side_ref[0, 0]
    partner = strips_ref[end_places(0, side)[1], 0:4, :]
    cross = cross_ref[...]
    top = jnp.where(side == 0, cross, partner)
    bottom = jnp.where(side == 0, partner, cross)
    for value, ref in enumerate((wz_ref, w_ref)):
        for line in range(lines):
            ref[line * piece : (line + 1) * piece, :] = strips_ref[
                end_places(line, side)[0], value * piece : (value + 1) * piece, :
            ]
        ref[0:2, :] = ref[0:2, :] + top[2 * value : 2 * value + 2]
        ref[rows - 2 :, :] = ref[rows - 2 :, :] + bottom[2 * value : 2 * value + 2]
    prefire = prefire_ref[...]
    filled = (wz_ref[...] + 16.0 * prefire) / (w_ref[...] + 16.0)
    out_ref[...] = filled - prefire


def per_device(cells, heights, weights, dest, counts, prefire_elevation):
    lines, columns, rows = (lax.axis_size(a) for a in ("line", "tile", ROW))
    blocks, points = cells.shape
    tile_rows, tile_cols = prefire_elevation.shape
    here = columns * CAPACITY
    f32 = jnp.float32
    piece = tile_rows // lines

    side = lax.axis_index("side").astype(jnp.int32).reshape(1, 1)
    packed = call(
        lambda *refs: pack_kernel(rows, columns, tile_cols, *refs),
        jax.ShapeDtypeStruct((rows, 3 * here, points), f32),
        [SMEM_SPEC, HBM_SPEC, SMEM_SPEC, HBM_SPEC, HBM_SPEC, HBM_SPEC],
        (2 * rows * here * blocks * 4 * points, 4 * 6 * rows * here * points),
        [
            pltpu.VMEM((1, blocks), jnp.int32),
            pltpu.VMEM((blocks, points), jnp.int32),
            pltpu.VMEM((blocks, points), f32),
            pltpu.VMEM((blocks, points), f32),
            pltpu.SemaphoreType.DMA((4,)),
        ],
        params=WHOLE_PARAMS,
    )(side, dest.reshape(1, blocks), counts.reshape(1, 1), cells, heights, weights)
    arrived = lax.all_to_all(
        packed,
        EVERY,
        split_axis=0,
        concat_axis=0,
        tiled=True,
        axis_index_groups=row_groups(lines, columns, rows),
    )

    tall = tile_rows + 16
    slot = 2 * piece + 8
    parts = call(
        lambda *refs: strip_kernel(lines, columns, tile_rows, tile_cols, *refs),
        jax.ShapeDtypeStruct((lines * columns, slot, tile_cols), f32),
        [VMEM_SPEC],
        (4 * rows * here * points * tile_rows * tile_cols, 4 * 4 * rows * here * points),
        [
            pltpu.VMEM((rows, here, points), f32),
            pltpu.VMEM((rows, here, points), f32),
            pltpu.VMEM((2, columns, tile_rows, tile_cols), f32),
            pltpu.VMEM((2, tall, tile_cols), f32),
            pltpu.VMEM((2, tall, tile_cols), f32),
        ],
    )(arrived)
    gathered = lax.all_to_all(
        parts,
        EVERY,
        split_axis=0,
        concat_axis=0,
        tiled=True,
        axis_index_groups=strip_groups(columns, rows),
    )

    strips, cross = call(
        gather_kernel,
        [
            jax.ShapeDtypeStruct((2 * lines, 2 * piece, tile_cols), f32),
            jax.ShapeDtypeStruct((4, tile_cols), f32),
        ],
        [SMEM_SPEC, VMEM_SPEC],
        (lines * columns * slot * tile_cols, 4 * lines * columns * slot * tile_cols),
    )(side, gathered)
    swap = [(i, i + 1) for i in range(1, rows - 1, 2)]
    cross = lax.ppermute(cross, ROW, swap + [(j, i) for i, j in swap])
    strips = lax.all_to_all(
        strips,
        EVERY,
        split_axis=0,
        concat_axis=0,
        tiled=True,
        axis_index_groups=end_groups(columns, rows),
    )

    return call(
        finish_kernel,
        jax.ShapeDtypeStruct((tile_rows, tile_cols), f32),
        [SMEM_SPEC] + [VMEM_SPEC] * 3,
        (8 * tile_rows * tile_cols, 16 * tile_rows * tile_cols),
        [pltpu.VMEM((tile_rows, tile_cols), f32), pltpu.VMEM((tile_rows, tile_cols), f32)],
    )(side, strips, cross, prefire_elevation)


def solution(mesh):
    lines, columns, rows = (mesh.shape[a] for a in ("line", "tile", "row"))
    paired = Mesh(
        mesh.devices.reshape(lines, columns, rows // 2, 2), ("line", "tile", "pair", "side")
    )
    placed = (
        P(("line", "tile") + ROW, None),
        P(("line", "tile") + ROW, None),
        P(("line", "tile") + ROW, None),
        P(("line", "tile") + ROW),
        P("line", "tile", ROW),
        P(ROW, "tile"),
    )
    return jax.shard_map(
        per_device, mesh=paired, in_specs=placed, out_specs=P(ROW, "tile"), check_vma=False
    )
```

```python
import jax
import jax.numpy as jnp
from jax import lax
from jax.experimental import pallas as pl
from jax.experimental.pallas import tpu as pltpu
from jax.sharding import Mesh
from jax.sharding import PartitionSpec as P

VMEM_SPEC = pl.BlockSpec(memory_space=pltpu.VMEM)
HBM_SPEC = pl.BlockSpec(memory_space=pltpu.HBM)
SMEM_SPEC = pl.BlockSpec(memory_space=pltpu.SMEM)
PARAMS = pltpu.CompilerParams(vmem_limit_bytes=40 * 1024 * 1024)
WHOLE_PARAMS = pltpu.CompilerParams(vmem_limit_bytes=60 * 1024 * 1024)
CAPACITY = 2
ROW = ("pair", "side")
EVERY = ("line", "tile") + ROW
ROW_ORDER = [10, 0, 5, 11, 13, 6, 3, 14, 4, 12, 2, 9, 7, 15, 1, 8]
STRIP_ORDER = [27, 28, 29, 30, 31, 0, 1, 2, 3, 4, 5, 6, 7, 8, 9, 10, 11, 12, 13, 14, 15, 16, 17, 18, 19, 20, 21, 22, 23, 24, 25, 26]
END_ORDER = [0, 1, 2, 3, 4, 5, 6, 7]


def row_groups(lines, columns, rows):
    return [
        [(a * columns + b) * rows + z for z in ROW_ORDER]
        for a in range(lines)
        for b in range(columns)
    ]


def strip_groups(columns, rows):
    return [[m * rows + z for m in STRIP_ORDER] for z in range(rows)]


def end_groups(columns, rows):
    return [
        [(m // 2 * columns + b) * rows + 2 * p + m % 2 for m in END_ORDER]
        for b in range(columns)
        for p in range(rows // 2)
    ]


def call(kernel, out_shape, specs, cost, scratch=(), params=PARAMS):
    outs = jax.tree.map(lambda _: VMEM_SPEC, out_shape)
    return pl.pallas_call(
        kernel,
        out_shape=out_shape,
        in_specs=specs,
        out_specs=outs,
        scratch_shapes=list(scratch),
        compiler_params=params,
        cost_estimate=pl.CostEstimate(flops=cost[0], bytes_accessed=cost[1], transcendentals=0),
    )


def pack_kernel(rows, columns, tile_cols, *refs):
    _, dest_hbm, counts_ref, cells_hbm, heights_hbm, weights_hbm, out_ref = refs[:7]
    dest_ref, cells_ref, heights_ref, weights_ref, sems = refs[7:]
    copies = [
        pltpu.make_async_copy(source, target, sems.at[i])
        for i, (source, target) in enumerate(
            (
                (dest_hbm, dest_ref),
                (weights_hbm, weights_ref),
                (heights_hbm, heights_ref),
                (cells_hbm, cells_ref),
            )
        )
    ]
    for copy in copies:
        copy.start()
    copies[0].wait()
    blocks = cells_ref.shape[0]
    points = cells_ref.shape[1]
    here = columns * CAPACITY
    slots = rows * here
    dest = dest_ref[...]
    across = jnp.broadcast_to(dest.astype(jnp.float32), (blocks, blocks))
    down = across.T
    before = lax.broadcasted_iota(jnp.int32, (blocks, blocks), 0) < lax.broadcasted_iota(
        jnp.int32, (blocks, blocks), 1
    )
    same = jnp.where((across == down) & before, 1.0, 0.0)
    rank = jnp.sum(same, axis=0, keepdims=True).astype(jnp.int32)
    tile_row = dest % rows
    place = tile_row
    for position, row in enumerate(ROW_ORDER):
        place = jnp.where(tile_row == row, position, place)
    slot = place * here + (dest // rows) * CAPACITY + rank
    live = lax.broadcasted_iota(jnp.int32, (1, blocks), 1) < counts_ref[0, 0]
    slot = jnp.where(live, slot, slots)
    move = jnp.where(
        lax.broadcasted_iota(jnp.int32, (slots, blocks), 0) == slot, 1.0, 0.0
    ).astype(jnp.bfloat16)
    for copy in copies[1:]:
        copy.wait()
    weights = weights_ref[...]
    cells = cells_ref[...]
    payload = jnp.concatenate(
        [
            (weights * heights_ref[...]).astype(jnp.bfloat16),
            weights.astype(jnp.bfloat16),
            (cells // tile_cols).astype(jnp.float32).astype(jnp.bfloat16),
            (cells % tile_cols).astype(jnp.float32).astype(jnp.bfloat16),
        ],
        axis=1,
    )
    moved = jnp.dot(move, payload, preferred_element_type=jnp.float32)
    out_ref[:, 0:here, :] = moved[:, 0:points].reshape(rows, here, points)
    out_ref[:, here : 2 * here, :] = moved[:, points : 2 * points].reshape(rows, here, points)
    cell = moved[:, 2 * points : 3 * points] * tile_cols + moved[:, 3 * points :]
    out_ref[:, 2 * here :, :] = cell.reshape(rows, here, points)


def strip_kernel(lines, columns, tile_rows, tile_cols, in_ref, out_ref, *scratch):
    row_ref, col_ref, held_ref, near_ref, far_ref = scratch
    sources, held, points = in_ref.shape
    here = held // 3
    piece = tile_rows // lines
    first, end = 8, 8 + tile_rows
    cells = in_ref[:, 2 * here :, :].astype(jnp.int32)
    row_ref[...] = (cells // tile_cols).astype(jnp.float32)
    col_ref[...] = (cells % tile_cols).astype(jnp.float32)
    row_ids = lax.broadcasted_iota(jnp.int32, (tile_rows, points), 0)
    row_ids = row_ids.astype(jnp.float32).astype(jnp.bfloat16)
    col_ids = lax.broadcasted_iota(jnp.int32, (tile_cols, points), 0)
    col_ids = col_ids.astype(jnp.float32).astype(jnp.bfloat16)
    zero = jnp.zeros((tile_rows, points), jnp.bfloat16)
    one_col = jnp.ones((tile_cols, points), jnp.bfloat16)
    zero_col = jnp.zeros((tile_cols, points), jnp.bfloat16)
    lane = lax.broadcasted_iota(jnp.int32, (tile_rows, tile_cols), 1)
    blank = jnp.zeros((tile_rows, tile_cols), jnp.float32)
    margin = jnp.zeros((2, 8, tile_cols), jnp.float32)
    for ref in (near_ref, far_ref):
        ref[:, 0:first, :] = margin
        ref[:, end:, :] = margin

    def spread(ref, source, at, count):
        line = ref[source, pl.ds(at, 1), :]
        piece_rows = jnp.broadcast_to(line, (16, points)).astype(jnp.bfloat16)
        return jnp.concatenate([piece_rows] * (count // 16), axis=0)

    def add_up(column):
        total = jnp.zeros((2 * tile_rows, tile_cols), jnp.float32)
        for source in range(0, sources, 2):
            lefts, rights = [], []
            for s in (source, source + 1):
                for k in range(CAPACITY):
                    at = column * CAPACITY + k
                    hit = spread(row_ref, s, at, tile_rows) == row_ids
                    wz = spread(in_ref, s, at, tile_rows)
                    w = spread(in_ref, s, here + at, tile_rows)
                    lefts.append(
                        jnp.concatenate([jnp.where(hit, wz, zero), jnp.where(hit, w, zero)], axis=0)
                    )
                    rights.append(
                        jnp.where(spread(col_ref, s, at, tile_cols) == col_ids, one_col, zero_col)
                    )
            total = total + lax.dot_general(
                jnp.concatenate(lefts, axis=1),
                jnp.concatenate(rights, axis=1),
                (((1,), (1,)), ((), ())),
                preferred_element_type=jnp.float32,
            )
        for value in range(2):
            held_ref[value, column] = total[value * tile_rows : (value + 1) * tile_rows, :]

    def turned(value, column):
        if column < 0 or column >= columns:
            return blank, blank, blank, blank
        x = held_ref[value, column]
        return tuple(pltpu.roll(x, s, 1) for s in (1, 2, tile_cols - 1, tile_cols - 2))

    def filter_column(value, column, before, here, after):
        x = held_ref[value, column]
        one = jnp.where(lane < 1, before[0], here[0]) + jnp.where(
            lane >= tile_cols - 1, after[2], here[2]
        )
        two = jnp.where(lane < 2, before[1], here[1]) + jnp.where(
            lane >= tile_cols - 2, after[3], here[3]
        )
        same = 2.0 * x + one + 0.25 * two
        near_ref[value, first:end, :] = x + 0.5 * one + 0.2 * two
        far_ref[value, first:end, :] = 0.25 * x + 0.2 * one + 0.125 * two

        def near(at, count):
            return near_ref[value, at : at + count, :]

        def far(at, count):
            return far_ref[value, at : at + count, :]

        inner = (
            same
            + near(first - 1, tile_rows)
            + near(first + 1, tile_rows)
            + far(first - 2, tile_rows)
            + far(first + 2, tile_rows)
        )
        outer = jnp.concatenate(
            [
                far(first, 1),
                near(first, 1) + far(first + 1, 1),
                near(end - 1, 1) + far(end - 2, 1),
                far(end - 1, 1),
            ],
            axis=0,
        )
        base = 2 * piece + 2 * value
        for line in range(lines):
            at = STRIP_ORDER.index(line * columns + column)
            out_ref[at, value * piece : (value + 1) * piece, :] = inner[
                line * piece : (line + 1) * piece, :
            ]
            out_ref[at, base : base + 2, :] = outer[0:2]
            out_ref[at, base + 4 : base + 6, :] = outer[2:4]

    add_up(0)
    before = [turned(value, -1) for value in range(2)]
    here_now = [turned(value, 0) for value in range(2)]
    for column in range(columns):
        if column + 1 < columns:
            add_up(column + 1)
        after = [turned(value, column + 1) for value in range(2)]
        for value in range(2):
            filter_column(value, column, before[value], here_now[value], after[value])
        before, here_now = here_now, after


def end_places(line, side):
    lower, upper = END_ORDER.index(2 * line), END_ORDER.index(2 * line + 1)
    return jnp.where(side == 0, lower, upper), jnp.where(side == 0, upper, lower)


def gather_kernel(side_ref, parts_ref, strips_ref, cross_ref):
    sources = parts_ref.shape[0]
    ends, both, tile_cols = strips_ref.shape
    total = parts_ref[0]
    for source in range(1, sources):
        total = total + parts_ref[source]
    above = total[both : both + 4]
    below = total[both + 4 :]
    side = side_ref[0, 0]
    lower = side == 0
    partner = jnp.concatenate(
        [jnp.where(lower, below, above), jnp.zeros((both - 4, tile_cols), jnp.float32)], axis=0
    )
    for line in range(ends // 2):
        here, there = end_places(line, side)
        strips_ref[here] = total[:both]
        strips_ref[there] = partner
    cross_ref[...] = jnp.where(lower, above, below)


def finish_kernel(side_ref, strips_ref, cross_ref, prefire_ref, out_ref, wz_ref, w_ref):
    ends, both, _ = strips_ref.shape
    lines = ends // 2
    piece = both // 2
    rows = lines * piece
    side = side_ref[0, 0]
    partner = strips_ref[end_places(0, side)[1], 0:4, :]
    cross = cross_ref[...]
    top = jnp.where(side == 0, cross, partner)
    bottom = jnp.where(side == 0, partner, cross)
    for value, ref in enumerate((wz_ref, w_ref)):
        for line in range(lines):
            ref[line * piece : (line + 1) * piece, :] = strips_ref[
                end_places(line, side)[0], value * piece : (value + 1) * piece, :
            ]
        ref[0:2, :] = ref[0:2, :] + top[2 * value : 2 * value + 2]
        ref[rows - 2 :, :] = ref[rows - 2 :, :] + bottom[2 * value : 2 * value + 2]
    prefire = prefire_ref[...]
    filled = (wz_ref[...] + 16.0 * prefire) / (w_ref[...] + 16.0)
    out_ref[...] = filled - prefire


def per_device(cells, heights, weights, dest, counts, prefire_elevation):
    lines, columns, rows = (lax.axis_size(a) for a in ("line", "tile", ROW))
    blocks, points = cells.shape
    tile_rows, tile_cols = prefire_elevation.shape
    here = columns * CAPACITY
    f32 = jnp.float32
    piece = tile_rows // lines

    side = lax.axis_index("side").astype(jnp.int32).reshape(1, 1)
    packed = call(
        lambda *refs: pack_kernel(rows, columns, tile_cols, *refs),
        jax.ShapeDtypeStruct((rows, 3 * here, points), f32),
        [SMEM_SPEC, HBM_SPEC, SMEM_SPEC, HBM_SPEC, HBM_SPEC, HBM_SPEC],
        (2 * rows * here * blocks * 4 * points, 4 * 6 * rows * here * points),
        [
            pltpu.VMEM((1, blocks), jnp.int32),
            pltpu.VMEM((blocks, points), jnp.int32),
            pltpu.VMEM((blocks, points), f32),
            pltpu.VMEM((blocks, points), f32),
            pltpu.SemaphoreType.DMA((4,)),
        ],
        params=WHOLE_PARAMS,
    )(side, dest.reshape(1, blocks), counts.reshape(1, 1), cells, heights, weights)
    arrived = lax.all_to_all(
        packed,
        EVERY,
        split_axis=0,
        concat_axis=0,
        tiled=True,
        axis_index_groups=row_groups(lines, columns, rows),
    )

    tall = tile_rows + 16
    slot = 2 * piece + 8
    parts = call(
        lambda *refs: strip_kernel(lines, columns, tile_rows, tile_cols, *refs),
        jax.ShapeDtypeStruct((lines * columns, slot, tile_cols), f32),
        [VMEM_SPEC],
        (4 * rows * here * points * tile_rows * tile_cols, 4 * 4 * rows * here * points),
        [
            pltpu.VMEM((rows, here, points), f32),
            pltpu.VMEM((rows, here, points), f32),
            pltpu.VMEM((2, columns, tile_rows, tile_cols), f32),
            pltpu.VMEM((2, tall, tile_cols), f32),
            pltpu.VMEM((2, tall, tile_cols), f32),
        ],
    )(arrived)
    gathered = lax.all_to_all(
        parts,
        EVERY,
        split_axis=0,
        concat_axis=0,
        tiled=True,
        axis_index_groups=strip_groups(columns, rows),
    )

    strips, cross = call(
        gather_kernel,
        [
            jax.ShapeDtypeStruct((2 * lines, 2 * piece, tile_cols), f32),
            jax.ShapeDtypeStruct((4, tile_cols), f32),
        ],
        [SMEM_SPEC, VMEM_SPEC],
        (lines * columns * slot * tile_cols, 4 * lines * columns * slot * tile_cols),
    )(side, gathered)
    swap = [(i, i + 1) for i in range(1, rows - 1, 2)]
    cross = lax.ppermute(cross, ROW, swap + [(j, i) for i, j in swap])
    strips = lax.all_to_all(
        strips,
        EVERY,
        split_axis=0,
        concat_axis=0,
        tiled=True,
        axis_index_groups=end_groups(columns, rows),
    )

    return call(
        finish_kernel,
        jax.ShapeDtypeStruct((tile_rows, tile_cols), f32),
        [SMEM_SPEC] + [VMEM_SPEC] * 3,
        (8 * tile_rows * tile_cols, 16 * tile_rows * tile_cols),
        [pltpu.VMEM((tile_rows, tile_cols), f32), pltpu.VMEM((tile_rows, tile_cols), f32)],
    )(side, strips, cross, prefire_elevation)


def solution(mesh):
    lines, columns, rows = (mesh.shape[a] for a in ("line", "tile", "row"))
    paired = Mesh(
        mesh.devices.reshape(lines, columns, rows // 2, 2), ("line", "tile", "pair", "side")
    )
    placed = (
        P(("line", "tile") + ROW, None),
        P(("line", "tile") + ROW, None),
        P(("line", "tile") + ROW, None),
        P(("line", "tile") + ROW),
        P("line", "tile", ROW),
        P(ROW, "tile"),
    )
    return jax.shard_map(
        per_device, mesh=paired, in_specs=placed, out_specs=P(ROW, "tile"), check_vma=False
    )
```

```python
import jax
import jax.numpy as jnp
from jax import lax
from jax.experimental import pallas as pl
from jax.experimental.pallas import tpu as pltpu
from jax.sharding import Mesh
from jax.sharding import PartitionSpec as P

VMEM_SPEC = pl.BlockSpec(memory_space=pltpu.VMEM)
HBM_SPEC = pl.BlockSpec(memory_space=pltpu.HBM)
SMEM_SPEC = pl.BlockSpec(memory_space=pltpu.SMEM)
PARAMS = pltpu.CompilerParams(vmem_limit_bytes=40 * 1024 * 1024)
WHOLE_PARAMS = pltpu.CompilerParams(vmem_limit_bytes=60 * 1024 * 1024)
CAPACITY = 2
ROW = ("pair", "side")
EVERY = ("line", "tile") + ROW
ROW_ORDER = [10, 0, 5, 11, 13, 6, 3, 14, 4, 12, 2, 9, 7, 15, 1, 8]
STRIP_ORDER = [27, 28, 29, 30, 31, 0, 1, 2, 3, 4, 5, 6, 7, 8, 9, 10, 11, 12, 13, 14, 15, 16, 17, 18, 19, 20, 21, 22, 23, 24, 25, 26]
END_ORDER = [0, 1, 2, 3, 4, 5, 6, 7]


def row_groups(lines, columns, rows):
    return [
        [(a * columns + b) * rows + z for z in ROW_ORDER]
        for a in range(lines)
        for b in range(columns)
    ]


def strip_groups(columns, rows):
    return [[m * rows + z for m in STRIP_ORDER] for z in range(rows)]


def end_groups(columns, rows):
    return [
        [(m // 2 * columns + b) * rows + 2 * p + m % 2 for m in END_ORDER]
        for b in range(columns)
        for p in range(rows // 2)
    ]


def call(kernel, out_shape, specs, cost, scratch=(), params=PARAMS):
    outs = jax.tree.map(lambda _: VMEM_SPEC, out_shape)
    return pl.pallas_call(
        kernel,
        out_shape=out_shape,
        in_specs=specs,
        out_specs=outs,
        scratch_shapes=list(scratch),
        compiler_params=params,
        cost_estimate=pl.CostEstimate(flops=cost[0], bytes_accessed=cost[1], transcendentals=0),
    )


def pack_kernel(rows, columns, tile_cols, *refs):
    _, dest_hbm, counts_ref, cells_hbm, heights_hbm, weights_hbm, out_ref = refs[:7]
    dest_ref, cells_ref, heights_ref, weights_ref, sems = refs[7:]
    copies = [
        pltpu.make_async_copy(source, target, sems.at[i])
        for i, (source, target) in enumerate(
            (
                (dest_hbm, dest_ref),
                (weights_hbm, weights_ref),
                (heights_hbm, heights_ref),
                (cells_hbm, cells_ref),
            )
        )
    ]
    for copy in copies:
        copy.start()
    copies[0].wait()
    blocks = cells_ref.shape[0]
    points = cells_ref.shape[1]
    here = columns * CAPACITY
    slots = rows * here
    dest = dest_ref[...]
    across = jnp.broadcast_to(dest.astype(jnp.float32), (blocks, blocks))
    down = across.T
    before = lax.broadcasted_iota(jnp.int32, (blocks, blocks), 0) < lax.broadcasted_iota(
        jnp.int32, (blocks, blocks), 1
    )
    same = jnp.where((across == down) & before, 1.0, 0.0)
    rank = jnp.sum(same, axis=0, keepdims=True).astype(jnp.int32)
    tile_row = dest % rows
    place = tile_row
    for position, row in enumerate(ROW_ORDER):
        place = jnp.where(tile_row == row, position, place)
    slot = place * here + (dest // rows) * CAPACITY + rank
    live = lax.broadcasted_iota(jnp.int32, (1, blocks), 1) < counts_ref[0, 0]
    slot = jnp.where(live, slot, slots)
    move = jnp.where(
        lax.broadcasted_iota(jnp.int32, (slots, blocks), 0) == slot, 1.0, 0.0
    ).astype(jnp.bfloat16)
    for copy in copies[1:]:
        copy.wait()
    weights = weights_ref[...]
    cells = cells_ref[...]
    payload = jnp.concatenate(
        [
            (weights * heights_ref[...]).astype(jnp.bfloat16),
            weights.astype(jnp.bfloat16),
            (cells >> (tile_cols.bit_length() - 1)).astype(jnp.float32).astype(jnp.bfloat16),
            (cells & (tile_cols - 1)).astype(jnp.float32).astype(jnp.bfloat16),
        ],
        axis=1,
    )
    moved = jnp.dot(move, payload, preferred_element_type=jnp.float32)
    out_ref[:, 0:here, :] = moved[:, 0:points].reshape(rows, here, points)
    out_ref[:, here : 2 * here, :] = moved[:, points : 2 * points].reshape(rows, here, points)
    cell = moved[:, 2 * points : 3 * points] * tile_cols + moved[:, 3 * points :]
    out_ref[:, 2 * here :, :] = cell.reshape(rows, here, points)


def strip_kernel(lines, columns, tile_rows, tile_cols, in_ref, out_ref, *scratch):
    row_ref, col_ref, held_ref, near_ref, far_ref = scratch
    sources, held, points = in_ref.shape
    here = held // 3
    piece = tile_rows // lines
    first, end = 8, 8 + tile_rows
    cells = in_ref[:, 2 * here :, :].astype(jnp.int32)
    row_ref[...] = (cells >> (tile_cols.bit_length() - 1)).astype(jnp.float32)
    col_ref[...] = (cells & (tile_cols - 1)).astype(jnp.float32)
    row_ids = lax.broadcasted_iota(jnp.int32, (tile_rows, points), 0)
    row_ids = row_ids.astype(jnp.float32).astype(jnp.bfloat16)
    col_ids = lax.broadcasted_iota(jnp.int32, (tile_cols, points), 0)
    col_ids = col_ids.astype(jnp.float32).astype(jnp.bfloat16)
    zero = jnp.zeros((tile_rows, points), jnp.bfloat16)
    one_col = jnp.ones((tile_cols, points), jnp.bfloat16)
    zero_col = jnp.zeros((tile_cols, points), jnp.bfloat16)
    lane = lax.broadcasted_iota(jnp.int32, (tile_rows, tile_cols), 1)
    blank = jnp.zeros((tile_rows, tile_cols), jnp.float32)
    margin = jnp.zeros((2, 8, tile_cols), jnp.float32)
    for ref in (near_ref, far_ref):
        ref[:, 0:first, :] = margin
        ref[:, end:, :] = margin

    def spread(ref, source, at, count):
        line = ref[source, pl.ds(at, 1), :]
        return jnp.broadcast_to(line, (count, points)).astype(jnp.bfloat16)

    def add_up(column):
        total = jnp.zeros((2 * tile_rows, tile_cols), jnp.float32)
        for source in range(0, sources, 2):
            lefts, rights = [], []
            for s in (source, source + 1):
                for k in range(CAPACITY):
                    at = column * CAPACITY + k
                    hit = spread(row_ref, s, at, tile_rows) == row_ids
                    wz = spread(in_ref, s, at, tile_rows)
                    w = spread(in_ref, s, here + at, tile_rows)
                    lefts.append(
                        jnp.concatenate([jnp.where(hit, wz, zero), jnp.where(hit, w, zero)], axis=0)
                    )
                    rights.append(
                        jnp.where(spread(col_ref, s, at, tile_cols) == col_ids, one_col, zero_col)
                    )
            total = total + lax.dot_general(
                jnp.concatenate(lefts, axis=1),
                jnp.concatenate(rights, axis=1),
                (((1,), (1,)), ((), ())),
                preferred_element_type=jnp.float32,
            )
        for value in range(2):
            held_ref[value, column] = total[value * tile_rows : (value + 1) * tile_rows, :]

    def turned(value, column):
        if column < 0 or column >= columns:
            return blank, blank, blank, blank
        x = held_ref[value, column]
        return tuple(pltpu.roll(x, s, 1) for s in (1, 2, tile_cols - 1, tile_cols - 2))

    def filter_column(value, column, before, here, after):
        x = held_ref[value, column]
        one = jnp.where(lane < 1, before[0], here[0]) + jnp.where(
            lane >= tile_cols - 1, after[2], here[2]
        )
        two = jnp.where(lane < 2, before[1], here[1]) + jnp.where(
            lane >= tile_cols - 2, after[3], here[3]
        )
        same = 2.0 * x + one + 0.25 * two
        near_ref[value, first:end, :] = x + 0.5 * one + 0.2 * two
        far_ref[value, first:end, :] = 0.25 * x + 0.2 * one + 0.125 * two

        def near(at, count):
            return near_ref[value, at : at + count, :]

        def far(at, count):
            return far_ref[value, at : at + count, :]

        inner = (
            same
            + near(first - 1, tile_rows)
            + near(first + 1, tile_rows)
            + far(first - 2, tile_rows)
            + far(first + 2, tile_rows)
        )
        outer = jnp.concatenate(
            [
                far(first, 1),
                near(first, 1) + far(first + 1, 1),
                near(end - 1, 1) + far(end - 2, 1),
                far(end - 1, 1),
            ],
            axis=0,
        )
        base = 2 * piece + 2 * value
        for line in range(lines):
            at = STRIP_ORDER.index(line * columns + column)
            out_ref[at, value * piece : (value + 1) * piece, :] = inner[
                line * piece : (line + 1) * piece, :
            ]
            out_ref[at, base : base + 2, :] = outer[0:2]
            out_ref[at, base + 4 : base + 6, :] = outer[2:4]

    add_up(0)
    before = [turned(value, -1) for value in range(2)]
    here_now = [turned(value, 0) for value in range(2)]
    for column in range(columns):
        if column + 1 < columns:
            add_up(column + 1)
        after = [turned(value, column + 1) for value in range(2)]
        for value in range(2):
            filter_column(value, column, before[value], here_now[value], after[value])
        before, here_now = here_now, after


def end_places(line, side):
    lower, upper = END_ORDER.index(2 * line), END_ORDER.index(2 * line + 1)
    return jnp.where(side == 0, lower, upper), jnp.where(side == 0, upper, lower)


def gather_kernel(side_ref, parts_ref, strips_ref, cross_ref):
    sources = parts_ref.shape[0]
    ends, both, tile_cols = strips_ref.shape
    total = parts_ref[0]
    for source in range(1, sources):
        total = total + parts_ref[source]
    above = total[both : both + 4]
    below = total[both + 4 :]
    side = side_ref[0, 0]
    lower = side == 0
    partner = jnp.concatenate(
        [jnp.where(lower, below, above), jnp.zeros((both - 4, tile_cols), jnp.float32)], axis=0
    )
    for line in range(ends // 2):
        here, there = end_places(line, side)
        strips_ref[here] = total[:both]
        strips_ref[there] = partner
    cross_ref[...] = jnp.where(lower, above, below)


def finish_kernel(side_ref, strips_ref, cross_ref, prefire_ref, out_ref, wz_ref, w_ref):
    ends, both, _ = strips_ref.shape
    lines = ends // 2
    piece = both // 2
    rows = lines * piece
    side = side_ref[0, 0]
    partner = strips_ref[end_places(0, side)[1], 0:4, :]
    cross = cross_ref[...]
    top = jnp.where(side == 0, cross, partner)
    bottom = jnp.where(side == 0, partner, cross)
    for value, ref in enumerate((wz_ref, w_ref)):
        for line in range(lines):
            ref[line * piece : (line + 1) * piece, :] = strips_ref[
                end_places(line, side)[0], value * piece : (value + 1) * piece, :
            ]
        ref[0:2, :] = ref[0:2, :] + top[2 * value : 2 * value + 2]
        ref[rows - 2 :, :] = ref[rows - 2 :, :] + bottom[2 * value : 2 * value + 2]
    prefire = prefire_ref[...]
    filled = (wz_ref[...] + 16.0 * prefire) / (w_ref[...] + 16.0)
    out_ref[...] = filled - prefire


def per_device(cells, heights, weights, dest, counts, prefire_elevation):
    lines, columns, rows = (lax.axis_size(a) for a in ("line", "tile", ROW))
    blocks, points = cells.shape
    tile_rows, tile_cols = prefire_elevation.shape
    here = columns * CAPACITY
    f32 = jnp.float32
    piece = tile_rows // lines

    side = lax.axis_index("side").astype(jnp.int32).reshape(1, 1)
    packed = call(
        lambda *refs: pack_kernel(rows, columns, tile_cols, *refs),
        jax.ShapeDtypeStruct((rows, 3 * here, points), f32),
        [SMEM_SPEC, HBM_SPEC, SMEM_SPEC, HBM_SPEC, HBM_SPEC, HBM_SPEC],
        (2 * rows * here * blocks * 4 * points, 4 * 6 * rows * here * points),
        [
            pltpu.VMEM((1, blocks), jnp.int32),
            pltpu.VMEM((blocks, points), jnp.int32),
            pltpu.VMEM((blocks, points), f32),
            pltpu.VMEM((blocks, points), f32),
            pltpu.SemaphoreType.DMA((4,)),
        ],
        params=WHOLE_PARAMS,
    )(side, dest.reshape(1, blocks), counts.reshape(1, 1), cells, heights, weights)
    arrived = lax.all_to_all(
        packed,
        EVERY,
        split_axis=0,
        concat_axis=0,
        tiled=True,
        axis_index_groups=row_groups(lines, columns, rows),
    )

    tall = tile_rows + 16
    slot = 2 * piece + 8
    parts = call(
        lambda *refs: strip_kernel(lines, columns, tile_rows, tile_cols, *refs),
        jax.ShapeDtypeStruct((lines * columns, slot, tile_cols), f32),
        [VMEM_SPEC],
        (4 * rows * here * points * tile_rows * tile_cols, 4 * 4 * rows * here * points),
        [
            pltpu.VMEM((rows, here, points), f32),
            pltpu.VMEM((rows, here, points), f32),
            pltpu.VMEM((2, columns, tile_rows, tile_cols), f32),
            pltpu.VMEM((2, tall, tile_cols), f32),
            pltpu.VMEM((2, tall, tile_cols), f32),
        ],
    )(arrived)
    gathered = lax.all_to_all(
        parts,
        EVERY,
        split_axis=0,
        concat_axis=0,
        tiled=True,
        axis_index_groups=strip_groups(columns, rows),
    )

    strips, cross = call(
        gather_kernel,
        [
            jax.ShapeDtypeStruct((2 * lines, 2 * piece, tile_cols), f32),
            jax.ShapeDtypeStruct((4, tile_cols), f32),
        ],
        [SMEM_SPEC, VMEM_SPEC],
        (lines * columns * slot * tile_cols, 4 * lines * columns * slot * tile_cols),
    )(side, gathered)
    swap = [(i, i + 1) for i in range(1, rows - 1, 2)]
    cross = lax.ppermute(cross, ROW, swap + [(j, i) for i, j in swap])
    strips = lax.all_to_all(
        strips,
        EVERY,
        split_axis=0,
        concat_axis=0,
        tiled=True,
        axis_index_groups=end_groups(columns, rows),
    )

    return call(
        finish_kernel,
        jax.ShapeDtypeStruct((tile_rows, tile_cols), f32),
        [SMEM_SPEC] + [VMEM_SPEC] * 3,
        (8 * tile_rows * tile_cols, 16 * tile_rows * tile_cols),
        [pltpu.VMEM((tile_rows, tile_cols), f32), pltpu.VMEM((tile_rows, tile_cols), f32)],
    )(side, strips, cross, prefire_elevation)


def solution(mesh):
    lines, columns, rows = (mesh.shape[a] for a in ("line", "tile", "row"))
    paired = Mesh(
        mesh.devices.reshape(lines, columns, rows // 2, 2), ("line", "tile", "pair", "side")
    )
    placed = (
        P(("line", "tile") + ROW, None),
        P(("line", "tile") + ROW, None),
        P(("line", "tile") + ROW, None),
        P(("line", "tile") + ROW),
        P("line", "tile", ROW),
        P(ROW, "tile"),
    )
    return jax.shard_map(
        per_device, mesh=paired, in_specs=placed, out_specs=P(ROW, "tile"), check_vma=False
    )
```
